512 devices in a mesh: lon: 32 (over y, x_lo, core), lat: 16 (over z, x_hi).
Axes of the slice: x: 4 (x_hi: 2, x_lo: 2; x = x_hi * 2 + x_lo), y: 8, z: 8, core: 2. Of those that a mesh axis runs over, the one named last changes fastest.
Arguments:
- height_old: float32 [4096, 2048], P('lon', 'lat'), may hold values from -6 to 6
- height_now: float32 [4096, 2048], P('lon', 'lat'), may hold values from -6 to 6
- zonal_old: float32 [4096, 2048], P('lon', 'lat'), may hold values from -6 to 6
- zonal_now: float32 [4096, 2048], P('lon', 'lat'), may hold values from -6 to 6
- meridional_old: float32 [4096, 2048], P('lon', 'lat'), may hold values from -6 to 6
- meridional_now: float32 [4096, 2048], P('lon', 'lat'), may hold values from -6 to 6
- ocean_depth: float32 [4096, 2048], P('lon', 'lat'), may hold values from 0.2 to 1
- land_sea: int32 [4096, 2048], P('lon', 'lat'), may hold values 0 or 1
- metric_factor: float32 [2048], P('lat'), may hold values from 0.5 to 2
- coriolis: float32 [2048], P('lat'), may hold values from -0.5 to 0.5
- implicit_weight: float32 [2048], replicated, may hold values from 150 to 40000
- source_longitude: int32 [512], replicated, may hold values from 0 to 4095
- source_latitude: int32 [512], replicated, may hold values from 0 to 2047
- source_amplitude: float32 [512], replicated, may hold values from -24 to 24
Outputs:
- height_final: float32 [4096, 2048], P('lon', 'lat')
- zonal_final: float32 [4096, 2048], P('lon', 'lat')
- meridional_final: float32 [4096, 2048], P('lon', 'lat')
The draws below stay inside these ranges and needn't reach their ends.
Inputs may be any that keep to these rules, and one draw needn't show every extreme that they name: `source_longitude`: cells may repeat.
All inputs are finite; a program needn't handle non-finite values. No bound on the sum of `land_sea` on one device may be relied on, other than what follows from the above.
Results may differ from the reference program's by a relative error of at most 0.0003.
Values sent between devices are 32-bit elements; how exact they have to be, the bound alone decides.
No kernel may reach another device: no remote copies, remote signals or barrier semaphores. Data moves between devices by JAX's collectives and lax.ppermute only.
A program may use at most 64 MiB of HBM per device.

```python
import math
import jax
import jax.numpy as jnp
from jax import lax

STEPS = 1
SOURCES = 512
NLON = 4096
NLAT = 2048


def draw_implicit_weight(key, part):
    phase_key, rough_key = jax.random.split(jax.random.fold_in(key, 211))
    north = jnp.arange(NLAT, dtype=jnp.float32) / NLAT
    phase = jax.random.uniform(phase_key, (), jnp.float32, 0.0, 2.0 * math.pi)
    wave = 0.5 + 0.5 * jnp.cos(4.0 * math.pi * north + phase)
    rough = jax.random.uniform(rough_key, (NLAT,), jnp.float32, 0.5, 1.0)
    level = 2.5 + 2.0 * wave
    return jnp.power(10.0, level).astype(jnp.float32) * rough


def draw_height_old(key, part):
    rough_key = jax.random.fold_in(jax.random.fold_in(key, 101), 0)
    return jax.random.truncated_normal(rough_key, -6.0, 6.0, (NLON, NLAT), jnp.float32)


def with_ends(array, own_key, least, largest):
    longest = array.shape.index(max(array.shape))
    spots = []
    for shift in (0, 1):
        where = [jax.random.randint(jax.random.fold_in(own_key, axis), (), 0, length) for axis, length in enumerate(array.shape)]
        where[longest] = (where[longest] + shift) % array.shape[longest]
        spots.append(tuple(where))
    return array.at[spots[0]].set(least).at[spots[1]].set(largest)


def levels(key, shape, cuts, least, largest):
    factor_of, own = 1.0, jax.random.fold_in(key, 6)
    for dim, blocks in cuts:
        steps = jnp.exp(jax.random.uniform(jax.random.fold_in(own, dim), (blocks,), jnp.float32, least / len(cuts), largest / len(cuts)))
        factor_of = factor_of * jnp.repeat(steps, shape[dim] // blocks).reshape([-1 if axis == dim else 1 for axis in range(len(shape))])
    return factor_of


def scatter_about(key, dims, spread, limit, cuts=(), held_as=jnp.bfloat16):
    drawn = jax.random.normal(key, dims, jnp.float32) * spread
    if len(cuts) > 0:
        drawn = levels(key, dims, cuts, -0.22, 0.18) * drawn
    return jnp.clip(drawn, min=-limit, max=limit).astype(held_as)


def setup_inputs(seed: int = 0) -> dict:
    arg_keys = jax.random.split(jax.random.key(seed), 15)
    return {
        "height_old": draw_height_old(jax.random.fold_in(arg_keys[14], 71), 0),
        "height_now": scatter_about(arg_keys[1], (NLON, NLAT), 1.0, 6.0, ((0, 32), (1, 16)), jnp.float32),
        "zonal_old": scatter_about(arg_keys[2], (NLON, NLAT), 1.0, 6.0, ((0, 32), (1, 16)), jnp.float32),
        "zonal_now": scatter_about(arg_keys[3], (NLON, NLAT), 1.0, 6.0, ((0, 32), (1, 16)), jnp.float32),
        "meridional_old": scatter_about(arg_keys[4], (NLON, NLAT), 1.0, 6.0, ((0, 32), (1, 16)), jnp.float32),
        "meridional_now": scatter_about(arg_keys[5], (NLON, NLAT), 1.0, 6.0, ((0, 32), (1, 16)), jnp.float32),
        "ocean_depth": jnp.clip(jnp.exp(math.log(1.0) - 1.609438 * jax.random.uniform(arg_keys[6], (NLON, NLAT), jnp.float32) ** levels(arg_keys[6], (NLON, NLAT), ((0, 32), (1, 16)), -0.2, 0.2)), 0.2, 1.0),
        "land_sea": with_ends((jax.random.randint(arg_keys[7], (NLON, NLAT), 0, 5) < 4).astype(jnp.int32), jax.random.fold_in(arg_keys[7], 1), 0, 1),
        "metric_factor": jnp.clip(jnp.exp(math.log(2.0) - 1.3862944 * jax.random.uniform(arg_keys[8], (NLAT,), jnp.float32) ** levels(arg_keys[8], (NLAT,), ((0, 16),), -0.2, 0.2)), 0.5, 2.0),
        "coriolis": jnp.clip(jax.random.uniform(arg_keys[9], (NLAT,), jnp.float32, -0.5, 0.5) * levels(arg_keys[9], (NLAT,), ((0, 16),), -0.4, 0.0), -0.5, 0.5),
        "implicit_weight": draw_implicit_weight(jax.random.fold_in(arg_keys[14], 71), 0),
        "source_longitude": with_ends(jax.random.randint(arg_keys[11], (SOURCES,), 0, NLON), jax.random.fold_in(arg_keys[11], 1), 0, NLON - 1).astype(jnp.int32),
        "source_latitude": with_ends(jax.random.randint(arg_keys[12], (SOURCES,), 0, NLAT), jax.random.fold_in(arg_keys[12], 1), 0, NLAT - 1).astype(jnp.int32),
        "source_amplitude": scatter_about(arg_keys[13], (SOURCES,), 4.0, 24.0, (), jnp.float32),
    }


COURANT = 0.25

def line_solve(rhs, weight):
    length = weight.shape[0]
    position = jnp.arange(length)
    lower = jnp.where(position > 0, -weight, jnp.zeros_like(weight))
    upper = jnp.where(position < length - 1, -weight, jnp.zeros_like(weight))
    middle = 1.0 + 2.0 * weight
    shape = rhs.shape
    solved = lax.linalg.tridiagonal_solve(jnp.broadcast_to(lower, shape), jnp.broadcast_to(middle, shape), jnp.broadcast_to(upper, shape), rhs[..., None])
    return solved[..., 0]

def east_diff(field):
    return jnp.roll(field, -1, 0) - jnp.roll(field, 1, 0)

def north_diff(field):
    upper = jnp.pad(field[:, 1:], ((0, 0), (0, 1)))
    lower = jnp.pad(field[:, :-1], ((0, 0), (1, 0)))
    return upper - lower

def reference(height_old, height_now, zonal_old, zonal_now, meridional_old, meridional_now, ocean_depth, land_sea, metric_factor, coriolis, implicit_weight, source_longitude, source_latitude, source_amplitude):
    wetness = land_sea.astype(height_old.dtype)
    metric = metric_factor[None, :]
    turning = coriolis[None, :]
    for _ in range(STEPS):
        flux_east = ocean_depth * wetness * zonal_now
        flux_north = ocean_depth * wetness * meridional_now
        interim = height_old - COURANT * (metric * east_diff(flux_east) + north_diff(flux_north))
        interim = interim.at[source_longitude, source_latitude].add(source_amplitude)
        zonal_next = wetness * (zonal_old - COURANT * metric * east_diff(height_now) + turning * meridional_now)
        meridional_next = wetness * (meridional_old - COURANT * north_diff(height_now) - turning * zonal_now)
        height_next = wetness * line_solve(interim, implicit_weight)
        height_old, zonal_old, meridional_old = (height_now, zonal_now, meridional_now)
        height_now, zonal_now, meridional_now = (height_next, zonal_next, meridional_next)
    return (height_now, zonal_now, meridional_now)
```

```python
import jax
import jax.numpy as jnp
from jax import lax
from jax.experimental import pallas as pl
from jax.experimental.pallas import tpu as pltpu
from jax.sharding import PartitionSpec as P

COURANT = 0.25
F32 = jnp.float32
BF16 = jnp.bfloat16
HIGH = lax.Precision.HIGHEST
VMEM = pl.BlockSpec(memory_space=pltpu.VMEM)
HBM = pl.BlockSpec(memory_space=pltpu.HBM)


def iota(shape, dim):
    return lax.broadcasted_iota(jnp.int32, shape, dim)


def dot(a, b, contract, precision=HIGH):
    return lax.dot_general(
        a, b, ((contract[:1], contract[1:]), ((), ())), precision=precision, preferred_element_type=F32
    )


def matmul2(x, y):
    a, b, c, d = x
    e, f, g, h = y
    return a * e + b * g, a * f + b * h, c * e + d * g, c * f + d * h


def product_scan(mats, axis, direction, rescale):
    shape = mats[0].shape
    size = shape[axis]
    place = iota(shape, axis)
    identity = (1.0, 0.0, 0.0, 1.0)
    step = 1
    while step < size:
        if direction == 1:
            keep, shift = place >= step, step
        else:
            keep, shift = place < size - step, size - step
        other = [jnp.where(keep, pltpu.roll(m, shift, axis), i) for m, i in zip(mats, identity)]
        mats = matmul2(mats, other)
        if rescale:
            factor = 1.0 / (mats[0] + mats[1] + mats[2] + mats[3])
            mats = tuple(m * factor for m in mats)
        step *= 2
    return mats


def lane(values, index):
    return jnp.broadcast_to(values[:, index : index + 1], values.shape)


def masked_product(values, low, high):
    row = iota(values.shape, 0)
    kept = jnp.where((row >= low) & (row < high), values, 1.0)
    out = kept[:8]
    for start in range(8, values.shape[0], 8):
        out = out * kept[start : start + 8]
    for step in (4, 2, 1):
        out = out * pltpu.roll(out, step, 0)
    return out


def pick(flag, yes, no):
    return jnp.where(jnp.full((8, 128), flag, jnp.int32) == 1, yes, no)


def rows_of(parts):
    row = iota((8, 128), 0)
    out = jnp.zeros((8, 128), F32)
    for index, part in enumerate(parts):
        out = jnp.where(row == index, part, out)
    return out


def prepare_kernel(*refs):
    sources, (interim_ref, total_ref, vectors_ref, mix_ref, take_ref, wet_ref, zonal_part_ref, meridional_part_ref, border_ref) = refs[:14], refs[14:23]
    held, rows_ref, arrived = refs[23:37], refs[37], refs[38]
    copies = [pltpu.make_async_copy(src, dst, arrived.at[i]) for i, (src, dst) in enumerate(zip(sources, held))]
    for copy in copies:
        copy.start()
    (
        weight_ref,
        lon_ref,
        lat_ref,
        amount_ref,
        height_old_ref,
        height_now_ref,
        zonal_old_ref,
        zonal_ref,
        meridional_old_ref,
        meridional_ref,
        depth_ref,
        land_ref,
        metric_ref,
        coriolis_ref,
    ) = held
    columns, rows = height_now_ref.shape
    blocks = weight_ref.shape[0]
    block = lax.axis_index("lat")
    first_east = lax.axis_index("lon") * columns
    first_north = block * rows

    copies[0].wait()
    c = 1.0 / weight_ref[...]
    one = jnp.ones_like(c)
    mats = (1.0 + c, one, c, one)
    up = product_scan(mats, 1, 1, False)
    down = product_scan(mats, 1, -1, False)
    up_all = tuple(lane(m, rows - 1) for m in up)
    down_all = tuple(lane(m, 0) for m in down)
    factor = 1.0 / (up_all[0] + up_all[1] + up_all[2] + up_all[3])
    ahead = product_scan(tuple(m * factor for m in up_all), 0, 1, True)
    factor = 1.0 / (down_all[0] + down_all[1] + down_all[2] + down_all[3])
    behind = product_scan(tuple(m * factor for m in down_all), 0, -1, True)
    row = iota(c.shape, 0)
    place = iota(c.shape, 1)
    rho = jnp.where(
        row == 0, 1.0, pltpu.roll((ahead[2] + ahead[3]) / (ahead[0] + ahead[1]), 1, 0)
    )
    sigma = jnp.where(
        row == blocks - 1,
        1.0,
        pltpu.roll((behind[2] + behind[3]) / (behind[0] + behind[1]), blocks - 1, 0),
    )
    p_after = up[0] + up[1] * rho
    q_before = down[0] + down[1] * sigma
    p = jnp.where(place == 0, 1.0, pltpu.roll(p_after, 1, 1))
    q = jnp.where(place == rows - 1, 1.0, pltpu.roll(q_before, rows - 1, 1))
    p_end = up_all[0] + up_all[1] * rho
    q_end = down_all[0] + down_all[1] * sigma
    scale = 1.0 / (up_all[2] + up_all[3] * rho + lane(p, rows - 1) * sigma)
    alpha = 1.0 / p_end
    beta = 1.0 / q_end
    c_below = jnp.where(row == 0, 0.0, pltpu.roll(lane(c, rows - 1), 1, 0))
    c_above = jnp.where(row == blocks - 1, 0.0, pltpu.roll(lane(c, 0), blocks - 1, 0))
    low_p = -COURANT * c_below * (1.0 - rho)
    low_q = -COURANT * c_below * q_end
    high_p = COURANT * c_above * p_end
    high_q = COURANT * c_above * (1.0 - sigma)
    stacked = (
        p * c,
        q * c,
        q * scale,
        p * scale,
        low_p * q * scale,
        high_q * p * scale,
        jnp.where(place == 0, low_p, jnp.where(place == rows - 1, high_p, 0.0)),
        jnp.where(place == 0, low_q, jnp.where(place == rows - 1, high_q, 0.0)),
    )
    for index, values in enumerate(stacked):
        rows_ref[index] = values
        vectors_ref[index : index + 1, :] = rows_ref[index, pl.ds(block, 1), :]

    for k in range(blocks.bit_length() - 1):
        size = 1 << k
        bit = (block >> k) & 1
        middle = ((block >> k) + 1 - bit) << k
        to_top = masked_product(alpha, middle - 1, middle + size - 1)
        to_bottom = masked_product(beta, middle - size + 1, middle + 1)
        own_up = masked_product(alpha, middle - 1, block)
        own_down = masked_product(beta, block + 1, middle + 1)
        is_first = (block == middle).astype(F32)
        is_last = (block == middle - 1).astype(F32)
        mine = rows_of((pick(bit, 1.0, to_top), pick(bit, to_bottom, 1.0), pick(bit, 1.0, 0.0), pick(bit, 0.0, 1.0)))
        theirs = rows_of((pick(bit, to_top, 1.0), pick(bit, 1.0, to_bottom), pick(bit, 0.0, 1.0), pick(bit, 1.0, 0.0)))
        take = rows_of((pick(bit, own_up, 0.0), pick(bit, 0.0, own_down), is_first, is_last))
        mix_ref[k, 0:4, :] = mine[0:4]
        mix_ref[k, 4:8, :] = theirs[0:4]
        take_ref[k, 0:4, :] = take[0:4]

    for copy in copies[1:]:
        copy.wait()
    shape = (columns, rows)
    lanes = iota(shape, 1)
    subs = iota(shape, 0)
    added = jnp.zeros(shape, F32)
    for chunk in range(lon_ref.shape[0]):
        amount = amount_ref[chunk : chunk + 1, :]
        here = lon_ref[chunk : chunk + 1, :] - first_east == subs
        there = jnp.where(lat_ref[chunk : chunk + 1, :] - first_north == subs, 1.0, 0.0).astype(BF16)
        for _ in range(3):
            part = amount.astype(BF16).astype(F32)
            amount = amount - part
            added += dot(jnp.where(here, part, 0.0).astype(BF16), there, (1, 1), None)

    wet = land_ref[...].astype(F32)
    depth = depth_ref[...] * wet
    flux_east = depth * zonal_ref[...]
    flux_north = depth * meridional_ref[...]
    across_east = jnp.where(subs == columns - 1, 0.0, pltpu.roll(flux_east, columns - 1, 0)) - jnp.where(
        subs == 0, 0.0, pltpu.roll(flux_east, 1, 0)
    )
    across_north = jnp.where(lanes == rows - 1, 0.0, pltpu.roll(flux_north, rows - 1, 1)) - jnp.where(
        lanes == 0, 0.0, pltpu.roll(flux_north, 1, 1)
    )
    interim = height_old_ref[...] - COURANT * (metric_ref[...] * across_east + across_north) + added
    interim_ref[...] = interim
    vectors = vectors_ref[...]
    border_ref[...] = flux_north[:, 0:1] * vectors[4:5, :] + flux_north[:, rows - 1 : rows] * vectors[5:6, :]

    height = height_now_ref[...]
    turning = coriolis_ref[...]
    across_east = jnp.where(subs == columns - 1, 0.0, pltpu.roll(height, columns - 1, 0)) - jnp.where(
        subs == 0, 0.0, pltpu.roll(height, 1, 0)
    )
    across_north = jnp.where(lanes == rows - 1, 0.0, pltpu.roll(height, rows - 1, 1)) - jnp.where(
        lanes == 0, 0.0, pltpu.roll(height, 1, 1)
    )
    wet_ref[...] = wet
    zonal_part_ref[...] = wet * (
        zonal_old_ref[...] - COURANT * metric_ref[...] * across_east + turning * meridional_ref[...]
    )
    meridional_part_ref[...] = wet * (
        meridional_old_ref[...] - COURANT * across_north - turning * zonal_ref[...]
    )

    eight = iota((8, rows), 0)
    along = iota((8, rows), 1)
    edges = pltpu.roll(vectors, 2, 0)
    on_interim = jnp.where(eight < 2, vectors, 0.0)
    on_flux = jnp.where(eight < 2, edges, 0.0)
    on_height = jnp.where(
        ((eight == 2) & (along == rows - 1)) | ((eight == 3) & (along == 0)), 1.0, 0.0
    )
    total = dot(on_interim, interim, (1, 1)) + dot(on_flux, flux_north, (1, 1))
    total += dot(on_height, height_now_ref[...], (1, 1))
    total_ref[...] = total[0:4]


def local_kernel(
    interim_ref, border_ref, vectors_ref, west_ref, east_ref, metric_ref, wet_ref, part_ref, solved_ref, zonal_ref
):
    shape = interim_ref.shape
    columns, rows = shape
    lanes = iota(shape, 1)
    subs = iota(shape, 0)
    wet = wet_ref[...]
    vectors = vectors_ref[...]
    outer = COURANT * metric_ref[...]
    at_west = jnp.where(subs == 0, outer, 0.0)
    at_east = jnp.where(subs == columns - 1, outer, 0.0)
    zonal_ref[...] = part_ref[...] + wet * (at_west * west_ref[0:1, :] - at_east * east_ref[0:1, :])
    interim = interim_ref[...] + at_west * west_ref[1:2, :] - at_east * east_ref[1:2, :]
    p_from = jnp.broadcast_to(vectors[0:1, :], shape).T
    q_from = jnp.broadcast_to(vectors[1:2, :], shape).T
    green = jnp.where(subs <= lanes, p_from * vectors[2:3, :], q_from * vectors[3:4, :])
    solved_ref[...] = wet * (dot(interim, green, (1, 0)) + border_ref[...])


def finish_kernel(taken_ref, vectors_ref, solved_ref, partial_ref, wet_ref, height_ref, meridional_ref):
    rows = vectors_ref.shape[1]
    four = iota((4, rows), 0)
    along = iota((4, rows), 1)
    taken = taken_ref[...]
    wet = wet_ref[...]
    solutions = jnp.where(four == 0, vectors_ref[2:3, :], jnp.where(four == 1, vectors_ref[3:4, :], 0.0))
    sides = jnp.where(
        (four == 2) & (along == 0),
        COURANT,
        jnp.where((four == 3) & (along == rows - 1), -COURANT, 0.0),
    )
    height_ref[...] = solved_ref[...] + wet * dot(taken, solutions, (0, 0))
    meridional_ref[...] = partial_ref[...] + wet * dot(taken, sides, (0, 0))


def call(kernel, shapes, in_specs, scratch=()):
    outs = [jax.ShapeDtypeStruct(shape, F32) for shape in shapes]
    return pl.pallas_call(
        kernel,
        out_shape=outs,
        in_specs=in_specs,
        out_specs=[VMEM] * len(outs),
        scratch_shapes=list(scratch),
        compiler_params=pltpu.CompilerParams(vmem_limit_bytes=54850 << 10 if kernel is prepare_kernel else 8 << 20),
    )


def per_device(
    height_old,
    height_now,
    zonal_old,
    zonal_now,
    meridional_old,
    meridional_now,
    ocean_depth,
    land_sea,
    metric_factor,
    coriolis,
    implicit_weight,
    source_longitude,
    source_latitude,
    source_amplitude,
):
    columns, rows = height_now.shape
    around = lax.axis_size("lon")
    blocks = lax.axis_size("lat")
    rounds = blocks.bit_length() - 1
    odd = lax.axis_index("lon") % 2 == 1
    metric = metric_factor[None, :]
    turning = coriolis[None, :]

    def outer(index):
        def row(values):
            return lax.slice_in_dim(values, index, index + 1, axis=0)

        flux = row(ocean_depth) * row(land_sea).astype(F32) * row(zonal_now)
        return jnp.concatenate([row(height_now), flux], axis=0)

    first, last = outer(0), outer(columns - 1)
    inner_pairs = [(i, i ^ 1) for i in range(around)]
    outer_pairs = [(i, (i + 1 if i % 2 else i - 1) % around) for i in range(around)]
    from_inner = lax.ppermute(jnp.where(odd, first, last), "lon", inner_pairs)
    from_outer = lax.ppermute(jnp.where(odd, last, first), "lon", outer_pairs)

    read = (
        implicit_weight.reshape(blocks, rows),
        source_longitude.reshape(-1, rows),
        source_latitude.reshape(-1, rows),
        source_amplitude.reshape(-1, rows),
        height_old,
        height_now,
        zonal_old,
        zonal_now,
        meridional_old,
        meridional_now,
        ocean_depth,
        land_sea,
        metric,
        turning,
    )
    block = (columns, rows)
    interim, total, vectors, mix, take, wet, zonal_part, meridional_part, border = call(
        prepare_kernel,
        [block, (4, columns), (8, rows), (rounds, 8, columns), (rounds, 4, columns), block, block, block, block],
        [HBM] * len(read),
        [pltpu.VMEM(x.shape, x.dtype) for x in read]
        + [pltpu.VMEM((8, blocks, rows), F32), pltpu.SemaphoreType.DMA((len(read),))],
    )(*read)

    east = jnp.where(odd, from_outer, from_inner)
    west = jnp.where(odd, from_inner, from_outer)
    weighted = COURANT * metric * vectors[0:2]
    at_west = jnp.sum(weighted * west[1:2], axis=1, keepdims=True)
    at_east = jnp.sum(weighted * east[1:2], axis=1, keepdims=True)
    along = lax.broadcasted_iota(jnp.int32, (2, columns), 1)
    change = jnp.where(along == 0, at_west, 0.0) - jnp.where(along == columns - 1, at_east, 0.0)
    group = jnp.concatenate([total[0:2] + change, total[2:4]], axis=0)

    solved, zonal_next = call(local_kernel, [block] * 2, [VMEM] * 8)(
        interim, border, vectors, west, east, metric, wet, zonal_part
    )

    taken = jnp.zeros_like(group)
    for k in range(rounds):
        size = 1 << k
        mask = size + size // 2 if k == rounds - 1 and k > 1 else size
        theirs = lax.ppermute(group, "lat", [(i, i ^ mask) for i in range(blocks)])
        taken = taken + take[k] * theirs
        group = mix[k, 0:4] * group + mix[k, 4:8] * theirs

    height_next, meridional_next = call(finish_kernel, [block] * 2, [VMEM] * 5)(
        taken, vectors, solved, meridional_part, wet
    )
    return height_next, zonal_next, meridional_next


def solution(mesh):
    grid = P("lon", "lat")
    placed = (grid,) * 8 + (P("lat"), P("lat"), P(), P(), P(), P())
    return jax.shard_map(
        per_device, mesh=mesh, in_specs=placed, out_specs=(grid, grid, grid), check_vma=False
    )
```

```python
import jax
import jax.numpy as jnp
from jax import lax
from jax.experimental import pallas as pl
from jax.experimental.pallas import tpu as pltpu
from jax.sharding import PartitionSpec as P

COURANT = 0.25
F32 = jnp.float32
PREPARE_LIMIT = 54800 << 10
BF16 = jnp.bfloat16
HIGH = lax.Precision.HIGHEST
VMEM = pl.BlockSpec(memory_space=pltpu.VMEM)
HBM = pl.BlockSpec(memory_space=pltpu.HBM)


def iota(shape, dim):
    return lax.broadcasted_iota(jnp.int32, shape, dim)


def dot(a, b, contract, precision=HIGH):
    return lax.dot_general(
        a, b, ((contract[:1], contract[1:]), ((), ())), precision=precision, preferred_element_type=F32
    )


def matmul2(x, y):
    a, b, c, d = x
    e, f, g, h = y
    return a * e + b * g, a * f + b * h, c * e + d * g, c * f + d * h


def product_scan(mats, axis, direction, rescale):
    shape = mats[0].shape
    size = shape[axis]
    place = iota(shape, axis)
    identity = (1.0, 0.0, 0.0, 1.0)
    step = 1
    while step < size:
        if direction == 1:
            keep, shift = place >= step, step
        else:
            keep, shift = place < size - step, size - step
        other = [jnp.where(keep, pltpu.roll(m, shift, axis), i) for m, i in zip(mats, identity)]
        mats = matmul2(mats, other)
        if rescale:
            factor = 1.0 / (mats[0] + mats[1] + mats[2] + mats[3])
            mats = tuple(m * factor for m in mats)
        step *= 2
    return mats


def lane(values, index):
    return jnp.broadcast_to(values[:, index : index + 1], values.shape)


def masked_product(values, low, high):
    row = iota(values.shape, 0)
    kept = jnp.where((row >= low) & (row < high), values, 1.0)
    out = kept[:8]
    for start in range(8, values.shape[0], 8):
        out = out * kept[start : start + 8]
    for step in (4, 2, 1):
        out = out * pltpu.roll(out, step, 0)
    return out


def select_rows(row, parts):
    out = jnp.zeros(row.shape, F32)
    for index, part in enumerate(parts):
        out = jnp.where(row == index, part, out)
    return out


def prepare_kernel(*refs):
    sources, results, held, rows_ref, arrived = refs[:14], refs[14:23], refs[23:37], refs[37], refs[38]
    copies = [pltpu.make_async_copy(src, dst, arrived.at[i]) for i, (src, dst) in enumerate(zip(sources, held))]
    for copy in copies:
        copy.start()
    (
        weight_ref,
        height_now_ref,
        zonal_ref,
        depth_ref,
        land_ref,
        lon_ref,
        lat_ref,
        amount_ref,
        meridional_ref,
        height_old_ref,
        metric_ref,
        coriolis_ref,
        zonal_old_ref,
        meridional_old_ref,
    ) = held
    (
        total_ref,
        vectors_ref,
        mix_ref,
        take_ref,
        wet_ref,
        zonal_part_ref,
        meridional_part_ref,
        green_ref,
        solved_ref,
    ) = results
    columns, rows = height_now_ref.shape
    blocks = weight_ref.shape[0]
    block = lax.axis_index("lat")
    first_east = lax.axis_index("lon") * columns
    first_north = block * rows

    copies[0].wait()
    c = 1.0 / weight_ref[...]
    one = jnp.ones_like(c)
    mats = (1.0 + c, one, c, one)
    up = product_scan(mats, 1, 1, False)
    down = product_scan(mats, 1, -1, False)
    up_all = tuple(lane(m, rows - 1) for m in up)
    down_all = tuple(lane(m, 0) for m in down)
    factor = 1.0 / (up_all[0] + up_all[1] + up_all[2] + up_all[3])
    ahead = product_scan(tuple(m * factor for m in up_all), 0, 1, True)
    factor = 1.0 / (down_all[0] + down_all[1] + down_all[2] + down_all[3])
    behind = product_scan(tuple(m * factor for m in down_all), 0, -1, True)
    row = iota(c.shape, 0)
    place = iota(c.shape, 1)
    rho = jnp.where(
        row == 0, 1.0, pltpu.roll((ahead[2] + ahead[3]) / (ahead[0] + ahead[1]), 1, 0)
    )
    sigma = jnp.where(
        row == blocks - 1,
        1.0,
        pltpu.roll((behind[2] + behind[3]) / (behind[0] + behind[1]), blocks - 1, 0),
    )
    p_after = up[0] + up[1] * rho
    q_before = down[0] + down[1] * sigma
    p = jnp.where(place == 0, 1.0, pltpu.roll(p_after, 1, 1))
    q = jnp.where(place == rows - 1, 1.0, pltpu.roll(q_before, rows - 1, 1))
    p_end = up_all[0] + up_all[1] * rho
    q_end = down_all[0] + down_all[1] * sigma
    scale = 1.0 / (up_all[2] + up_all[3] * rho + lane(p, rows - 1) * sigma)
    alpha = 1.0 / p_end
    beta = 1.0 / q_end
    c_below = jnp.where(row == 0, 0.0, pltpu.roll(lane(c, rows - 1), 1, 0))
    c_above = jnp.where(row == blocks - 1, 0.0, pltpu.roll(lane(c, 0), blocks - 1, 0))
    low_p = -COURANT * c_below * (1.0 - rho)
    low_q = -COURANT * c_below * q_end
    high_p = COURANT * c_above * p_end
    high_q = COURANT * c_above * (1.0 - sigma)
    stacked = (
        p * c,
        q * c,
        q * scale,
        p * scale,
        low_p * q * scale,
        high_q * p * scale,
        jnp.where(place == 0, low_p, jnp.where(place == rows - 1, high_p, 0.0)),
        jnp.where(place == 0, low_q, jnp.where(place == rows - 1, high_q, 0.0)),
    )
    for index, values in enumerate(stacked):
        rows_ref[index] = values
        vectors_ref[index : index + 1, :] = rows_ref[index, pl.ds(block, 1), :]

    eight = iota((8, rows), 0)
    for k in range(blocks.bit_length() - 1):
        size = 1 << k
        bit = (block >> k) & 1
        middle = ((block >> k) + 1 - bit) << k
        to_top = masked_product(alpha, middle - 1, middle + size - 1)
        to_bottom = masked_product(beta, middle - size + 1, middle + 1)
        own_up = masked_product(alpha, middle - 1, block) * bit.astype(F32)
        own_down = masked_product(beta, block + 1, middle + 1) * (1 - bit).astype(F32)
        is_first = (block == middle).astype(F32)
        is_last = (block == middle - 1).astype(F32)
        mix_ref[k] = select_rows(eight, (to_top, 1.0, 0.0, 1.0, 1.0, to_bottom, 1.0, 0.0))
        take_ref[k] = select_rows(eight, (own_up, 0.0, is_first, 0.0, 0.0, own_down, 0.0, is_last))

    for copy in copies[1:]:
        copy.wait()
    shape = (columns, rows)
    lanes = iota(shape, 1)
    subs = iota(shape, 0)
    added = jnp.zeros(shape, F32)
    for chunk in range(lon_ref.shape[0]):
        amount = amount_ref[chunk : chunk + 1, :]
        here = lon_ref[chunk : chunk + 1, :] - first_east == subs
        there = jnp.where(lat_ref[chunk : chunk + 1, :] - first_north == subs, 1.0, 0.0).astype(BF16)
        for _ in range(3):
            part = amount.astype(BF16).astype(F32)
            amount = amount - part
            added += dot(jnp.where(here, part, 0.0).astype(BF16), there, (1, 1), None)

    wet = land_ref[...].astype(F32)
    depth = depth_ref[...] * wet
    flux_east = depth * zonal_ref[...]
    flux_north = depth * meridional_ref[...]
    across_east = jnp.where(subs == columns - 1, 0.0, pltpu.roll(flux_east, columns - 1, 0)) - jnp.where(
        subs == 0, 0.0, pltpu.roll(flux_east, 1, 0)
    )
    across_north = jnp.where(lanes == rows - 1, 0.0, pltpu.roll(flux_north, rows - 1, 1)) - jnp.where(
        lanes == 0, 0.0, pltpu.roll(flux_north, 1, 1)
    )
    interim = height_old_ref[...] - COURANT * (metric_ref[...] * across_east + across_north) + added

    vectors = vectors_ref[...]
    p_from = jnp.broadcast_to(vectors[0:1, :], shape).T
    q_from = jnp.broadcast_to(vectors[1:2, :], shape).T
    green = jnp.where(subs <= lanes, p_from * vectors[2:3, :], q_from * vectors[3:4, :])
    green_ref[...] = green
    solved = dot(interim, green, (1, 0))
    solved += flux_north[:, 0:1] * vectors[4:5, :] + flux_north[:, rows - 1 : rows] * vectors[5:6, :]
    solved_ref[...] = wet * solved

    height = height_now_ref[...]
    turning = coriolis_ref[...]
    across_east = jnp.where(subs == columns - 1, 0.0, pltpu.roll(height, columns - 1, 0)) - jnp.where(
        subs == 0, 0.0, pltpu.roll(height, 1, 0)
    )
    across_north = jnp.where(lanes == rows - 1, 0.0, pltpu.roll(height, rows - 1, 1)) - jnp.where(
        lanes == 0, 0.0, pltpu.roll(height, 1, 1)
    )
    wet_ref[...] = wet
    zonal_part_ref[...] = wet * (
        zonal_old_ref[...] - COURANT * metric_ref[...] * across_east + turning * meridional_ref[...]
    )
    meridional_part_ref[...] = wet * (
        meridional_old_ref[...] - COURANT * across_north - turning * zonal_ref[...]
    )

    along = iota((8, rows), 1)
    edges = pltpu.roll(vectors, 2, 0)
    on_interim = jnp.where(eight < 2, vectors, 0.0)
    on_flux = jnp.where(eight < 2, edges, 0.0)
    on_height = jnp.where(
        ((eight == 2) & (along == rows - 1)) | ((eight == 3) & (along == 0)), 1.0, 0.0
    )
    total = dot(on_interim, interim, (1, 1)) + dot(on_flux, flux_north, (1, 1))
    total += dot(on_height, height_now_ref[...], (1, 1))
    total_ref[...] = total[0:4]


def finish_kernel(
    west_ref,
    east_ref,
    metric_ref,
    vectors_ref,
    green_ref,
    wet_ref,
    zonal_part_ref,
    meridional_part_ref,
    solved_ref,
    take_ref,
    *refs,
):
    gathered, (height_ref, zonal_ref, meridional_ref) = refs[:-3], refs[-3:]
    columns, rows = wet_ref.shape
    wet = wet_ref[...]
    outer = COURANT * metric_ref[...]
    eight = iota((8, rows), 0)
    along = iota((8, columns), 1)

    zonal_ref[...] = zonal_part_ref[...]
    last = columns - 1
    zonal_ref[0:1, :] += wet_ref[0:1, :] * outer * west_ref[0:1, :]
    zonal_ref[last:columns, :] -= wet_ref[last:columns, :] * outer * east_ref[0:1, :]

    halo = select_rows(eight, (0.0, 0.0, 0.0, 0.0, outer * west_ref[1:2, :], -outer * east_ref[1:2, :]))
    outer_rows = dot(halo, green_ref[...], (1, 0))

    taken = take_ref[0] * gathered[0][...]
    for k in range(1, len(gathered)):
        taken += take_ref[k] * gathered[k][...]
    taken += pltpu.roll(taken, 4, 0)
    onto = jnp.where(
        eight < 4, taken, jnp.where((eight == 4) & (along == 0) | (eight == 5) & (along == last), 1.0, 0.0)
    )
    heights = select_rows(
        eight, (vectors_ref[2:3, :], vectors_ref[3:4, :], 0.0, 0.0, outer_rows, outer_rows)
    )
    sides = jnp.where(
        (eight == 2) & (along == 0), COURANT, jnp.where((eight == 3) & (along == rows - 1), -COURANT, 0.0)
    )
    height_ref[...] = solved_ref[...] + wet * dot(onto, heights, (0, 0))
    meridional_ref[...] = meridional_part_ref[...] + wet * dot(onto, sides, (0, 0))


def call(kernel, shapes, in_specs, scratch=(), limit=8 << 20):
    outs = [jax.ShapeDtypeStruct(x.shape, x.dtype) for x in shapes]
    return pl.pallas_call(
        kernel,
        out_shape=outs,
        in_specs=in_specs,
        out_specs=[VMEM] * len(outs),
        scratch_shapes=list(scratch),
        compiler_params=pltpu.CompilerParams(vmem_limit_bytes=limit),
    )


def f32(*shape):
    return jax.ShapeDtypeStruct(shape, F32)


def per_device(
    height_old,
    height_now,
    zonal_old,
    zonal_now,
    meridional_old,
    meridional_now,
    ocean_depth,
    land_sea,
    metric_factor,
    coriolis,
    implicit_weight,
    source_longitude,
    source_latitude,
    source_amplitude,
):
    columns, rows = height_now.shape
    around = lax.axis_size("lon")
    blocks = lax.axis_size("lat")
    rounds = blocks.bit_length() - 1
    odd = lax.axis_index("lon") % 2 == 1

    metric = metric_factor[None, :]

    def outer(index):
        def row(values):
            return lax.slice_in_dim(values, index, index + 1, axis=0)

        flux = row(ocean_depth) * row(land_sea).astype(F32) * row(zonal_now)
        return jnp.concatenate([row(height_now), flux], axis=0)

    first, last = outer(0), outer(columns - 1)

    inner_pairs = [(i, i ^ 1) for i in range(around)]
    outer_pairs = [(i, (i + 1 if i % 2 else i - 1) % around) for i in range(around)]
    from_outer = lax.ppermute(jnp.where(odd, last, first), "lon", outer_pairs)
    from_inner = lax.ppermute(jnp.where(odd, first, last), "lon", inner_pairs)

    block = f32(columns, rows)
    read = (
        implicit_weight.reshape(blocks, rows),
        height_now,
        zonal_now,
        ocean_depth,
        land_sea,
        source_longitude.reshape(-1, rows),
        source_latitude.reshape(-1, rows),
        source_amplitude.reshape(-1, rows),
        meridional_now,
        height_old,
        metric,
        coriolis[None, :],
        zonal_old,
        meridional_old,
    )
    total, vectors, mix, take, wet, zonal_part, meridional_part, green, solved = call(
        prepare_kernel,
        [f32(4, columns), f32(8, rows), f32(rounds, 8, columns), f32(rounds, 8, columns)] + [block] * 5,
        [HBM] * len(read),
        [pltpu.VMEM(x.shape, x.dtype) for x in read]
        + [pltpu.VMEM((8, blocks, rows), F32), pltpu.SemaphoreType.DMA((len(read),))],
        PREPARE_LIMIT,
    )(*read)

    east = jnp.where(odd, from_outer, from_inner)
    west = jnp.where(odd, from_inner, from_outer)
    weighted = COURANT * metric * vectors[0:2]
    at_west = jnp.sum(weighted * west[1:2], axis=1, keepdims=True)
    at_east = jnp.sum(weighted * east[1:2], axis=1, keepdims=True)
    along = lax.broadcasted_iota(jnp.int32, (2, columns), 1)
    change = jnp.where(along == 0, at_west, 0.0) - jnp.where(along == columns - 1, at_east, 0.0)
    group = jnp.concatenate([total[0:2] + change, total[2:4]], axis=0)

    gathered = []
    for k in range(rounds):
        size = 1 << k
        mask = size + size // 2 if k == rounds - 1 and k > 1 else size
        pairs = [[i, i ^ mask] for i in range(blocks) if i < i ^ mask]
        both = lax.all_gather(group, "lat", axis=0, tiled=True, axis_index_groups=pairs)
        gathered.append(both)
        if k < rounds - 1:
            group = mix[k, 0:4] * both[0:4] + mix[k, 4:8] * both[4:8]

    height_next, zonal_next, meridional_next = call(finish_kernel, [block] * 3, [VMEM] * (10 + rounds))(
        west, east, metric, vectors, green, wet, zonal_part, meridional_part, solved, take, *gathered
    )
    return height_next, zonal_next, meridional_next


def solution(mesh):
    grid = P("lon", "lat")
    placed = (grid,) * 8 + (P("lat"), P("lat"), P(), P(), P(), P())
    return jax.shard_map(
        per_device, mesh=mesh, in_specs=placed, out_specs=(grid, grid, grid), check_vma=False
    )
```

```python
import jax
import jax.numpy as jnp
from jax import lax
from jax.experimental import pallas as pl
from jax.experimental.pallas import tpu as pltpu
from jax.sharding import PartitionSpec as P

COURANT = 0.25
F32 = jnp.float32
BF16 = jnp.bfloat16
HIGH = lax.Precision.HIGHEST
VMEM = pl.BlockSpec(memory_space=pltpu.VMEM)
HBM = pl.BlockSpec(memory_space=pltpu.HBM)
LIMIT = 8 << 20


def iota(shape, dim):
    return lax.broadcasted_iota(jnp.int32, shape, dim)


def dot(a, b, contract, precision=HIGH):
    return lax.dot_general(
        a, b, ((contract[:1], contract[1:]), ((), ())), precision=precision, preferred_element_type=F32
    )


def matmul2(x, y):
    a, b, c, d = x
    e, f, g, h = y
    return a * e + b * g, a * f + b * h, c * e + d * g, c * f + d * h


def product_scan(mats, axis, direction, rescale):
    shape = mats[0].shape
    size = shape[axis]
    place = iota(shape, axis)
    identity = (1.0, 0.0, 0.0, 1.0)
    step = 1
    while step < size:
        if direction == 1:
            keep, shift = place >= step, step
        else:
            keep, shift = place < size - step, size - step
        other = [jnp.where(keep, pltpu.roll(m, shift, axis), i) for m, i in zip(mats, identity)]
        mats = matmul2(mats, other)
        if rescale:
            factor = 1.0 / (mats[0] + mats[1] + mats[2] + mats[3])
            mats = tuple(m * factor for m in mats)
        step *= 2
    return mats


def lane(values, index):
    return jnp.broadcast_to(values[:, index : index + 1], values.shape)


def running_product(values, direction):
    size = values.shape[0]
    row = iota(values.shape, 0)
    step = 1
    while step < size:
        if direction == 1:
            keep, shift = row >= step, step
        else:
            keep, shift = row < size - step, size - step
        values = values * jnp.where(keep, pltpu.roll(values, shift, 0), 1.0)
        step *= 2
    return values


def differences(values, axis):
    size = values.shape[axis]
    place = iota(values.shape, axis)
    after = jnp.where(place == size - 1, 0.0, pltpu.roll(values, size - 1, axis))
    before = jnp.where(place == 0, 0.0, pltpu.roll(values, 1, axis))
    return after - before


def load(sources, held, arrived):
    copies = [pltpu.make_async_copy(src, dst, arrived.at[i]) for i, (src, dst) in enumerate(zip(sources, held))]
    for copy in copies:
        copy.start()
    return copies


def select_rows(row, parts):
    out = jnp.zeros(row.shape, F32)
    for index, part in enumerate(parts):
        out = jnp.where(row == index, part, out)
    return out


def sums_kernel(*refs):
    count = 11
    sources, refs = refs[:count], refs[count:]
    (own_ref, to_inner_ref, to_outer_ref, interim_ref, vectors_ref, alpha_ref, beta_ref), refs = refs[:7], refs[7:]
    held, rows_ref, arrived = refs[:count], refs[count], refs[count + 1]
    copies = load(sources, held, arrived)
    (
        weight_ref,
        height_now_ref,
        zonal_ref,
        depth_ref,
        land_ref,
        lon_ref,
        lat_ref,
        amount_ref,
        meridional_ref,
        height_old_ref,
        metric_ref,
    ) = held
    columns, rows = height_now_ref.shape
    blocks = weight_ref.shape[0]
    block = lax.axis_index("lat")
    first_east = lax.axis_index("lon") * columns
    first_north = block * rows

    copies[0].wait()
    c = 1.0 / weight_ref[...]
    one = jnp.ones_like(c)
    mats = (1.0 + c, one, c, one)
    up = product_scan(mats, 1, 1, False)
    down = product_scan(mats, 1, -1, False)
    up_all = tuple(lane(m, rows - 1) for m in up)
    down_all = tuple(lane(m, 0) for m in down)
    factor = 1.0 / (up_all[0] + up_all[1] + up_all[2] + up_all[3])
    ahead = product_scan(tuple(m * factor for m in up_all), 0, 1, True)
    factor = 1.0 / (down_all[0] + down_all[1] + down_all[2] + down_all[3])
    behind = product_scan(tuple(m * factor for m in down_all), 0, -1, True)
    row = iota(c.shape, 0)
    place = iota(c.shape, 1)
    rho = jnp.where(
        row == 0, 1.0, pltpu.roll((ahead[2] + ahead[3]) / (ahead[0] + ahead[1]), 1, 0)
    )
    sigma = jnp.where(
        row == blocks - 1,
        1.0,
        pltpu.roll((behind[2] + behind[3]) / (behind[0] + behind[1]), blocks - 1, 0),
    )
    p_after = up[0] + up[1] * rho
    q_before = down[0] + down[1] * sigma
    p = jnp.where(place == 0, 1.0, pltpu.roll(p_after, 1, 1))
    q = jnp.where(place == rows - 1, 1.0, pltpu.roll(q_before, rows - 1, 1))
    p_end = up_all[0] + up_all[1] * rho
    q_end = down_all[0] + down_all[1] * sigma
    scale = 1.0 / (up_all[2] + up_all[3] * rho + lane(p, rows - 1) * sigma)
    c_below = jnp.where(row == 0, 0.0, pltpu.roll(lane(c, rows - 1), 1, 0))
    c_above = jnp.where(row == blocks - 1, 0.0, pltpu.roll(lane(c, 0), blocks - 1, 0))
    low_p = -COURANT * c_below * (1.0 - rho)
    low_q = -COURANT * c_below * q_end
    high_p = COURANT * c_above * p_end
    high_q = COURANT * c_above * (1.0 - sigma)
    stacked = (
        p * c,
        q * c,
        q * scale,
        p * scale,
        low_p * q * scale,
        high_q * p * scale,
        jnp.where(place == 0, low_p, jnp.where(place == rows - 1, high_p, 0.0)),
        jnp.where(place == 0, low_q, jnp.where(place == rows - 1, high_q, 0.0)),
    )
    alpha_ref[...] = 1.0 / p_end
    beta_ref[...] = 1.0 / q_end
    for index, values in enumerate(stacked):
        rows_ref[index] = values
        vectors_ref[index : index + 1, :] = rows_ref[index, pl.ds(block, 1), :]

    for copy in copies[1:]:
        copy.wait()
    shape = (columns, rows)
    subs = iota(shape, 0)
    added = jnp.zeros(shape, F32)
    for chunk in range(lon_ref.shape[0]):
        amount = amount_ref[chunk : chunk + 1, :]
        here = lon_ref[chunk : chunk + 1, :] - first_east == subs
        there = jnp.where(lat_ref[chunk : chunk + 1, :] - first_north == subs, 1.0, 0.0).astype(BF16)
        for _ in range(3):
            part = amount.astype(BF16).astype(F32)
            amount = amount - part
            added += dot(jnp.where(here, part, 0.0).astype(BF16), there, (1, 1), None)

    depth = depth_ref[...] * land_ref[...].astype(F32)
    flux_east = depth * zonal_ref[...]
    flux_north = depth * meridional_ref[...]
    metric = metric_ref[...]
    interim = (
        height_old_ref[...]
        - COURANT * (metric * differences(flux_east, 0) + differences(flux_north, 1))
        + added
    )
    interim_ref[...] = interim

    eight = iota((8, rows), 0)
    along = iota((8, rows), 1)
    vectors = vectors_ref[...]
    edges = pltpu.roll(vectors, 2, 0)
    on_interim = jnp.where(eight < 2, vectors, 0.0)
    on_flux = jnp.where(eight < 2, edges, 0.0)
    on_height = jnp.where(
        ((eight == 2) & (along == rows - 1)) | ((eight == 3) & (along == 0)), 1.0, 0.0
    )
    total = dot(on_interim, interim, (1, 1)) + dot(on_flux, flux_north, (1, 1))
    total += dot(on_height, height_now_ref[...], (1, 1))
    own_ref[...] = total[0:4]

    last = columns - 1
    odd = jnp.full((8, columns), lax.axis_index("lon") & 1, jnp.int32) == 1
    line = iota((8, columns), 1)
    onto = COURANT * metric * vectors
    flux_first, flux_last = flux_east[0:1, :], flux_east[last:columns, :]
    to_west = jnp.where(line == last, -jnp.sum(onto * flux_first, axis=1, keepdims=True), 0.0)
    to_east = jnp.where(line == 0, jnp.sum(onto * flux_last, axis=1, keepdims=True), 0.0)
    to_west = jnp.where(eight < 2, to_west, jnp.where(eight == 2, height_now_ref[0:1, :], flux_first))
    to_east = jnp.where(eight < 2, to_east, jnp.where(eight == 2, height_now_ref[last:columns, :], flux_last))
    to_inner_ref[...] = jnp.where(odd, to_west, to_east)[0:4]
    to_outer_ref[...] = jnp.where(odd, to_east, to_west)[0:4]


def local_kernel(*refs):
    count = 9
    sources, refs = refs[:count], refs[count:]
    (interim_ref, vectors_ref, alpha_ref, beta_ref), refs = refs[:4], refs[4:]
    (wet_ref, zonal_part_ref, meridional_part_ref, green_ref, solved_ref, take_ref, outer_ref), refs = refs[:7], refs[7:]
    held, arrived = refs[:count], refs[count]
    copies = load(sources, held, arrived)
    (
        height_now_ref,
        zonal_ref,
        depth_ref,
        land_ref,
        meridional_ref,
        metric_ref,
        coriolis_ref,
        zonal_old_ref,
        meridional_old_ref,
    ) = held
    shape = height_now_ref.shape
    rows = shape[1]
    subs = iota(shape, 0)
    lanes = iota(shape, 1)
    blocks = alpha_ref.shape[0]
    block = lax.axis_index("lat")

    row = iota(alpha_ref.shape, 0)
    from_south = running_product(jnp.where(row < block, alpha_ref[...], 1.0), -1)
    from_north = running_product(jnp.where(row > block, beta_ref[...], 1.0), 1)
    weights = (
        jnp.where(row < block, from_south, 0.0),
        jnp.where(row > block, from_north, 0.0),
        jnp.where(row == block - 1, 1.0, 0.0),
        jnp.where(row == block + 1, 1.0, 0.0),
    )
    for source in range(blocks):
        for index, values in enumerate(weights):
            take_ref[source, index : index + 1, :] = values[source : source + 1, :]

    for copy in copies:
        copy.wait()
    wet = land_ref[...].astype(F32)
    flux_north = depth_ref[...] * wet * meridional_ref[...]

    vectors = vectors_ref[...]
    p_from = jnp.broadcast_to(vectors[0:1, :], shape).T
    q_from = jnp.broadcast_to(vectors[1:2, :], shape).T
    green = jnp.where(subs <= lanes, p_from * vectors[2:3, :], q_from * vectors[3:4, :])
    green_ref[...] = green
    solved = dot(interim_ref[...], green, (1, 0))
    solved += flux_north[:, 0:1] * vectors[4:5, :] + flux_north[:, rows - 1 : rows] * vectors[5:6, :]
    solved_ref[...] = wet * solved

    height = height_now_ref[...]
    outer_ref[...] = COURANT * metric_ref[...]
    turning = coriolis_ref[...]
    wet_ref[...] = wet
    zonal_part_ref[...] = wet * (
        zonal_old_ref[...] - COURANT * metric_ref[...] * differences(height, 0) + turning * meridional_ref[...]
    )
    meridional_part_ref[...] = wet * (
        meridional_old_ref[...] - COURANT * differences(height, 1) - turning * zonal_ref[...]
    )


def finish_kernel(
    received_ref,
    inner_ref,
    outer_ref,
    vectors_ref,
    green_ref,
    wet_ref,
    zonal_part_ref,
    meridional_part_ref,
    solved_ref,
    take_ref,
    height_ref,
    zonal_ref,
    meridional_ref,
):
    columns, rows = wet_ref.shape
    blocks = take_ref.shape[0]
    last = columns - 1
    wet = wet_ref[...]
    outer = outer_ref[...]
    eight = iota((8, rows), 0)
    along = iota((8, columns), 1)
    block = lax.axis_index("lat")
    parity = lax.axis_index("lon") & 1
    odd = jnp.full((4, columns), parity, jnp.int32) == 1
    at_own, at_other = (1 - parity) * blocks, parity * blocks

    inner = inner_ref[1 - parity]
    other = received_ref[at_other + block]
    west = jnp.where(odd, inner, other)
    east = jnp.where(odd, other, inner)
    zonal_ref[...] = zonal_part_ref[...]
    zonal_ref[0:1, :] += wet_ref[0:1, :] * outer * west[2:3, :]
    zonal_ref[last:columns, :] -= wet_ref[last:columns, :] * outer * east[2:3, :]
    halo = select_rows(eight, (0.0, 0.0, 0.0, 0.0, outer * west[3:4, :], -outer * east[3:4, :]))
    outer_rows = dot(halo, green_ref[...], (1, 0))

    sums = iota((4, columns), 0) < 2
    taken = jnp.zeros((4, columns), F32)
    for source in range(blocks):
        values = received_ref[at_own + source] + jnp.where(sums, received_ref[at_other + source], 0.0)
        taken += take_ref[source] * values
    onto = jnp.concatenate([taken, jnp.zeros_like(taken)], axis=0)
    onto = jnp.where((eight == 4) & (along == 0) | (eight == 5) & (along == last), 1.0, onto)
    heights = select_rows(
        eight, (vectors_ref[2:3, :], vectors_ref[3:4, :], 0.0, 0.0, outer_rows, outer_rows)
    )
    sides = jnp.where(
        (eight == 2) & (along == 0), COURANT, jnp.where((eight == 3) & (along == rows - 1), -COURANT, 0.0)
    )
    height_ref[...] = solved_ref[...] + wet * dot(onto, heights, (0, 0))
    meridional_ref[...] = meridional_part_ref[...] + wet * dot(onto, sides, (0, 0))


def call(kernel, outs, in_specs, scratch=()):
    return pl.pallas_call(
        kernel,
        out_shape=outs,
        in_specs=in_specs,
        out_specs=[VMEM] * len(outs),
        scratch_shapes=list(scratch),
        compiler_params=pltpu.CompilerParams(vmem_limit_bytes=LIMIT),
    )


def loading(read):
    return [pltpu.VMEM(x.shape, x.dtype) for x in read], pltpu.SemaphoreType.DMA((len(read),))


def kept(*shape):
    return pltpu.VMEM(shape, F32)


def per_device(
    height_old,
    height_now,
    zonal_old,
    zonal_now,
    meridional_old,
    meridional_now,
    ocean_depth,
    land_sea,
    metric_factor,
    coriolis,
    implicit_weight,
    source_longitude,
    source_latitude,
    source_amplitude,
):
    columns, rows = height_now.shape
    around = lax.axis_size("lon")
    blocks = lax.axis_size("lat")
    odd = lax.axis_index("lon") % 2 == 1

    def pinned(values):
        return pltpu.with_memory_space_constraint(values, pltpu.HBM)

    height_now, zonal_now, ocean_depth, land_sea, meridional_now, metric = (
        pinned(x) for x in (height_now, zonal_now, ocean_depth, land_sea, meridional_now, metric_factor[None, :])
    )
    read = (
        pinned(implicit_weight.reshape(blocks, rows)),
        height_now,
        zonal_now,
        ocean_depth,
        land_sea,
        pinned(source_longitude.reshape(-1, rows)),
        pinned(source_latitude.reshape(-1, rows)),
        pinned(source_amplitude.reshape(-1, rows)),
        meridional_now,
        pinned(height_old),
        metric,
    )
    held, arrived = loading(read)
    own, to_inner, to_outer, interim, vectors, alpha, beta = call(
        sums_kernel,
        [kept(4, columns), kept(4, columns), kept(4, columns), kept(columns, rows)]
        + [kept(8, rows), kept(blocks, rows), kept(blocks, rows)],
        [HBM] * len(read),
        [*held, pltpu.VMEM((8, blocks, rows), F32), arrived],
    )(*read)

    pairs = [[i, i + 1] for i in range(0, around, 2)]
    inner = lax.all_gather(to_inner, "lon", axis=0, axis_index_groups=pairs)
    from_inner = jnp.where(odd, inner[0], inner[1])
    own = jnp.concatenate([own[0:2] + from_inner[0:2], own[2:4]], axis=0)

    groups = [
        [lon * blocks + lat for lon in (first, (first + 1) % around) for lat in range(blocks)]
        for first in range(1, around, 2)
    ]
    parts = (blocks, 4, columns)
    low = jnp.broadcast_to(jnp.where(odd, own, to_outer), parts)
    high = jnp.broadcast_to(jnp.where(odd, to_outer, own), parts)
    received = lax.all_to_all(
        jnp.concatenate([low, high], axis=0), ("lon", "lat"), 0, 0, axis_index_groups=groups, tiled=True
    )

    read = (
        height_now,
        zonal_now,
        ocean_depth,
        land_sea,
        meridional_now,
        metric,
        pinned(coriolis[None, :]),
        pinned(zonal_old),
        pinned(meridional_old),
    )
    held, arrived = loading(read)
    wet, zonal_part, meridional_part, green, solved, take, outer = call(
        local_kernel,
        [kept(columns, rows)] * 5 + [kept(blocks, 4, rows), kept(1, rows)],
        [HBM] * len(read) + [VMEM] * 4,
        [*held, arrived],
    )(*read, interim, vectors, alpha, beta)

    block = jax.ShapeDtypeStruct((columns, rows), F32)
    return tuple(
        call(finish_kernel, [block] * 3, [VMEM] * 10)(
            received, inner, outer, vectors, green, wet, zonal_part, meridional_part, solved, take
        )
    )


def solution(mesh):
    grid = P("lon", "lat")
    placed = (grid,) * 8 + (P("lat"), P("lat"), P(), P(), P(), P())
    return jax.shard_map(
        per_device, mesh=mesh, in_specs=placed, out_specs=(grid, grid, grid), check_vma=False
    )
```

```python
import jax
import jax.numpy as jnp
from jax import lax
from jax.experimental import pallas as pl
from jax.experimental.pallas import tpu as pltpu
from jax.sharding import PartitionSpec as P

COURANT = 0.25
F32 = jnp.float32
BF16 = jnp.bfloat16
HIGH = lax.Precision.HIGHEST
VMEM = pl.BlockSpec(memory_space=pltpu.VMEM)
HBM = pl.BlockSpec(memory_space=pltpu.HBM)
LIMIT = 8 << 20


def iota(shape, dim):
    return lax.broadcasted_iota(jnp.int32, shape, dim)


def dot(a, b, contract, precision=HIGH):
    return lax.dot_general(
        a, b, ((contract[:1], contract[1:]), ((), ())), precision=precision, preferred_element_type=F32
    )


def matmul2(x, y):
    a, b, c, d = x
    e, f, g, h = y
    return a * e + b * g, a * f + b * h, c * e + d * g, c * f + d * h


def product_scan(mats, axis, direction, rescale):
    shape = mats[0].shape
    size = shape[axis]
    place = iota(shape, axis)
    identity = (1.0, 0.0, 0.0, 1.0)
    step = 1
    while step < size:
        reach = [step * i for i in range(1, min(4, size // step))]
        others = []
        for distance in reach:
            if direction == 1:
                keep, shift = place >= distance, distance
            else:
                keep, shift = place < size - distance, size - distance
            others.append([jnp.where(keep, pltpu.roll(m, shift, axis), i) for m, i in zip(mats, identity)])
        factors = [mats, *others]
        while len(factors) > 1:
            factors = [matmul2(x, y) for x, y in zip(factors[::2], factors[1::2])]
        mats = factors[0]
        if rescale:
            factor = 1.0 / (mats[0] + mats[1] + mats[2] + mats[3])
            mats = tuple(m * factor for m in mats)
        step *= len(reach) + 1
    return mats


def lane(values, index):
    return jnp.broadcast_to(values[:, index : index + 1], values.shape)


def running_product(values, direction):
    size = values.shape[0]
    row = iota(values.shape, 0)
    step = 1
    while step < size:
        if direction == 1:
            keep, shift = row >= step, step
        else:
            keep, shift = row < size - step, size - step
        values = values * jnp.where(keep, pltpu.roll(values, shift, 0), 1.0)
        step *= 2
    return values


def differences(values, axis):
    size = values.shape[axis]
    place = iota(values.shape, axis)
    after = jnp.where(place == size - 1, 0.0, pltpu.roll(values, size - 1, axis))
    before = jnp.where(place == 0, 0.0, pltpu.roll(values, 1, axis))
    return after - before


def load(sources, held, arrived):
    copies = [pltpu.make_async_copy(src, dst, arrived.at[i]) for i, (src, dst) in enumerate(zip(sources, held))]
    for copy in copies:
        copy.start()
    return copies


def select_rows(row, parts):
    out = jnp.zeros(row.shape, F32)
    for index, part in enumerate(parts):
        out = jnp.where(row == index, part, out)
    return out


def thirds(values):
    high = values.astype(BF16).astype(F32)
    rest = values - high
    middle = rest.astype(BF16).astype(F32)
    return high, middle, rest - middle


def sums_dot(a, b):
    size = a.shape[0]
    left = jnp.concatenate(thirds(a), axis=0).astype(BF16)
    out = jnp.zeros((size, b.shape[0]), F32)
    for skip, part in enumerate(thirds(b)):
        product = dot(left, part.astype(BF16), (1, 1), None)
        for index in range(3 - skip):
            out += product[index * size : (index + 1) * size]
    return out


def sums_kernel(*refs):
    count = 11
    sources, refs = refs[:count], refs[count:]
    (own_ref, to_inner_ref, to_outer_ref, interim_ref, vectors_ref, alpha_ref, beta_ref), refs = refs[:7], refs[7:]
    held, rows_ref, arrived = refs[:count], refs[count], refs[count + 1]
    copies = load(sources, held, arrived)
    (
        weight_ref,
        height_now_ref,
        zonal_ref,
        depth_ref,
        land_ref,
        lon_ref,
        lat_ref,
        amount_ref,
        meridional_ref,
        height_old_ref,
        metric_ref,
    ) = held
    columns, rows = height_now_ref.shape
    blocks = weight_ref.shape[0]
    block = lax.axis_index("lat")
    first_east = lax.axis_index("lon") * columns
    first_north = block * rows

    for copy in copies:
        copy.wait()
    c = 1.0 / weight_ref[...]
    one = jnp.ones_like(c)
    mats = (1.0 + c, one, c, one)
    up = product_scan(mats, 1, 1, False)
    down = product_scan(mats, 1, -1, False)
    up_all = tuple(lane(m, rows - 1) for m in up)
    down_all = tuple(lane(m, 0) for m in down)
    factor = 1.0 / (up_all[0] + up_all[1] + up_all[2] + up_all[3])
    ahead = product_scan(tuple(m * factor for m in up_all), 0, 1, True)
    factor = 1.0 / (down_all[0] + down_all[1] + down_all[2] + down_all[3])
    behind = product_scan(tuple(m * factor for m in down_all), 0, -1, True)
    row = iota(c.shape, 0)
    place = iota(c.shape, 1)
    rho = jnp.where(
        row == 0, 1.0, pltpu.roll((ahead[2] + ahead[3]) / (ahead[0] + ahead[1]), 1, 0)
    )
    sigma = jnp.where(
        row == blocks - 1,
        1.0,
        pltpu.roll((behind[2] + behind[3]) / (behind[0] + behind[1]), blocks - 1, 0),
    )
    p_after = up[0] + up[1] * rho
    q_before = down[0] + down[1] * sigma
    p = jnp.where(place == 0, 1.0, pltpu.roll(p_after, 1, 1))
    q = jnp.where(place == rows - 1, 1.0, pltpu.roll(q_before, rows - 1, 1))
    p_end = up_all[0] + up_all[1] * rho
    q_end = down_all[0] + down_all[1] * sigma
    scale = 1.0 / (up_all[2] + up_all[3] * rho + lane(p, rows - 1) * sigma)
    c_below = jnp.where(row == 0, 0.0, pltpu.roll(lane(c, rows - 1), 1, 0))
    c_above = jnp.where(row == blocks - 1, 0.0, pltpu.roll(lane(c, 0), blocks - 1, 0))
    low_p = -COURANT * c_below * (1.0 - rho)
    low_q = -COURANT * c_below * q_end
    high_p = COURANT * c_above * p_end
    high_q = COURANT * c_above * (1.0 - sigma)
    stacked = (
        p * c,
        q * c,
        q * scale,
        p * scale,
        low_p * q * scale,
        high_q * p * scale,
        jnp.where(place == 0, low_p, jnp.where(place == rows - 1, high_p, 0.0)),
        jnp.where(place == 0, low_q, jnp.where(place == rows - 1, high_q, 0.0)),
    )
    alpha_ref[...] = 1.0 / p_end
    beta_ref[...] = 1.0 / q_end
    for index, values in enumerate(stacked):
        rows_ref[index] = values
        vectors_ref[index : index + 1, :] = rows_ref[index, pl.ds(block, 1), :]

    shape = (columns, rows)
    subs = iota(shape, 0)
    added = jnp.zeros(shape, F32)
    parts = thirds(amount_ref[...])
    chunks = range(lon_ref.shape[0])
    here = [lon_ref[i : i + 1, :] - first_east == subs for i in chunks]
    there = jnp.concatenate(
        [jnp.where(lat_ref[i : i + 1, :] - first_north == subs, 1.0, 0.0) for i in chunks], axis=1
    ).astype(BF16)
    for part in parts:
        amounts = jnp.concatenate([jnp.where(here[i], part[i : i + 1, :], 0.0) for i in chunks], axis=1)
        added += dot(amounts.astype(BF16), there, (1, 1), None)

    depth = depth_ref[...] * land_ref[...].astype(F32)
    flux_east = depth * zonal_ref[...]
    flux_north = depth * meridional_ref[...]
    metric = metric_ref[...]
    interim = (
        height_old_ref[...]
        - COURANT * (metric * differences(flux_east, 0) + differences(flux_north, 1))
        + added
    )
    interim_ref[...] = interim

    eight = iota((8, rows), 0)
    along = iota((8, rows), 1)
    vectors = vectors_ref[...]
    on_interim = jnp.where(eight < 2, vectors, 0.0)
    on_edges = jnp.where(eight < 2, pltpu.roll(vectors, 2, 0), 0.0)
    on_edges += jnp.where((eight == 2) & (along == 1) | (eight == 3) & (along == 2), 1.0, 0.0)
    lanes = iota(shape, 1)
    edges = jnp.where((lanes == 0) | (lanes == rows - 1), flux_north, pltpu.roll(height_now_ref[...], 2, 1))
    total = sums_dot(
        jnp.concatenate([on_interim, on_edges], axis=1), jnp.concatenate([interim, edges], axis=1)
    )
    own_ref[...] = total[0:4]

    last = columns - 1
    odd = jnp.full((8, columns), lax.axis_index("lon") & 1, jnp.int32) == 1
    line = iota((8, columns), 1)
    onto = COURANT * metric * vectors
    flux_first, flux_last = flux_east[0:1, :], flux_east[last:columns, :]
    to_west = jnp.where(line == last, -jnp.sum(onto * flux_first, axis=1, keepdims=True), 0.0)
    to_east = jnp.where(line == 0, jnp.sum(onto * flux_last, axis=1, keepdims=True), 0.0)
    to_west = jnp.where(eight < 2, to_west, jnp.where(eight == 2, height_now_ref[0:1, :], flux_first))
    to_east = jnp.where(eight < 2, to_east, jnp.where(eight == 2, height_now_ref[last:columns, :], flux_last))
    to_inner_ref[...] = jnp.where(odd, to_west, to_east)[0:4]
    to_outer_ref[...] = jnp.where(odd, to_east, to_west)[0:4]


def pack_kernel(own_ref, inner_ref, to_outer_ref, send_ref):
    blocks = send_ref.shape[0] // 2
    block = lax.axis_index("lat")
    parity = lax.axis_index("lon") & 1
    at_own, at_outer = (1 - parity) * blocks, parity * blocks
    own = own_ref[...]
    row = iota(own.shape, 0)
    own += jnp.where(row < 2, inner_ref[1 - parity], 0.0)
    outer = to_outer_ref[...]
    own_up = jnp.concatenate([own[0:1], own[2:3]], axis=0)
    own_down = jnp.concatenate([own[1:2], own[3:4]], axis=0)
    outer_up = jnp.concatenate([outer[0:1], jnp.zeros_like(outer[0:1])], axis=0)
    outer_down = jnp.concatenate([outer[1:2], jnp.zeros_like(outer[0:1])], axis=0)
    for target in range(blocks):
        north = jnp.full(own_up.shape, (block < target).astype(jnp.int32), jnp.int32) == 1
        send_ref[at_own + target] = jnp.where(north, own_up, own_down)
        send_ref[at_outer + target] = jnp.where(north, outer_up, outer_down)
    send_ref[at_outer + block] = outer[2:4]


def local_kernel(*refs):
    count = 9
    sources, refs = refs[:count], refs[count:]
    (interim_ref, vectors_ref, alpha_ref, beta_ref), refs = refs[:4], refs[4:]
    (wet_ref, zonal_part_ref, meridional_part_ref, green_ref, solved_ref, take_ref, outer_ref), refs = refs[:7], refs[7:]
    held, arrived = refs[:count], refs[count]
    copies = load(sources, held, arrived)
    (
        height_now_ref,
        zonal_ref,
        depth_ref,
        land_ref,
        meridional_ref,
        metric_ref,
        coriolis_ref,
        zonal_old_ref,
        meridional_old_ref,
    ) = held
    shape = height_now_ref.shape
    rows = shape[1]
    subs = iota(shape, 0)
    lanes = iota(shape, 1)
    blocks = alpha_ref.shape[0]
    block = lax.axis_index("lat")

    row = iota(alpha_ref.shape, 0)
    from_south = running_product(jnp.where(row < block, alpha_ref[...], 1.0), -1)
    from_north = running_product(jnp.where(row > block, beta_ref[...], 1.0), 1)
    weights = (
        jnp.where(row < block, from_south, 0.0),
        jnp.where(row == block - 1, 1.0, 0.0),
        jnp.where(row > block, from_north, 0.0),
        jnp.where(row == block + 1, 1.0, 0.0),
    )
    for source in range(blocks):
        for index, values in enumerate(weights):
            take_ref[source, index : index + 1, :] = values[source : source + 1, :]

    for copy in copies:
        copy.wait()
    wet = land_ref[...].astype(F32)
    flux_north = depth_ref[...] * wet * meridional_ref[...]

    vectors = vectors_ref[...]
    p_from = jnp.broadcast_to(vectors[0:1, :], shape).T
    q_from = jnp.broadcast_to(vectors[1:2, :], shape).T
    green = jnp.where(subs <= lanes, p_from * vectors[2:3, :], q_from * vectors[3:4, :])
    for index, part in enumerate(thirds(green)):
        green_ref[index] = part.astype(BF16)
    solved = dot(interim_ref[...], green, (1, 0))
    solved += flux_north[:, 0:1] * vectors[4:5, :] + flux_north[:, rows - 1 : rows] * vectors[5:6, :]
    solved_ref[...] = wet * solved

    height = height_now_ref[...]
    outer_ref[...] = COURANT * metric_ref[...]
    turning = coriolis_ref[...]
    wet_ref[...] = wet
    zonal_part_ref[...] = wet * (
        zonal_old_ref[...] - COURANT * metric_ref[...] * differences(height, 0) + turning * meridional_ref[...]
    )
    meridional_part_ref[...] = wet * (
        meridional_old_ref[...] - COURANT * differences(height, 1) - turning * zonal_ref[...]
    )


def finish_kernel(
    received_ref,
    inner_ref,
    outer_ref,
    vectors_ref,
    green_ref,
    wet_ref,
    zonal_part_ref,
    meridional_part_ref,
    solved_ref,
    take_ref,
    height_ref,
    zonal_ref,
    meridional_ref,
):
    columns, rows = wet_ref.shape
    blocks = take_ref.shape[0]
    last = columns - 1
    wet = wet_ref[...]
    outer = outer_ref[...]
    eight = iota((8, rows), 0)
    along = iota((8, columns), 1)
    block = lax.axis_index("lat")
    parity = lax.axis_index("lon") & 1
    at_own, at_other = (1 - parity) * blocks, parity * blocks

    inner = inner_ref[1 - parity][2:4]
    other = received_ref[at_other + block]
    odd = jnp.full(other.shape, parity, jnp.int32) == 1
    west = jnp.where(odd, inner, other)
    east = jnp.where(odd, other, inner)
    zonal_ref[...] = zonal_part_ref[...]
    zonal_ref[0:1, :] += wet_ref[0:1, :] * outer * west[0:1, :]
    zonal_ref[last:columns, :] -= wet_ref[last:columns, :] * outer * east[0:1, :]

    halo = select_rows(eight, (0.0, 0.0, 0.0, 0.0, outer * west[1:2, :], -outer * east[1:2, :]))
    left = jnp.concatenate(thirds(halo), axis=0).astype(BF16)
    outer_rows = jnp.zeros((8, rows), F32)
    for skip in range(3):
        product = dot(left, green_ref[skip], (1, 0), None)
        for index in range(3 - skip):
            outer_rows += product[8 * index : 8 * index + 8]

    south = jnp.zeros(other.shape, F32)
    north = jnp.zeros(other.shape, F32)
    for source in range(blocks):
        values = received_ref[at_own + source] + received_ref[at_other + source]
        take = take_ref[source]
        south += take[0:2] * values
        north += take[2:4] * values
    onto = jnp.concatenate([south, north, jnp.zeros((4, columns), F32)], axis=0)
    onto = jnp.where((eight == 4) & (along == 0) | (eight == 5) & (along == last), 1.0, onto)
    heights = select_rows(
        eight, (vectors_ref[2:3, :], 0.0, vectors_ref[3:4, :], 0.0, outer_rows, outer_rows)
    )
    sides = jnp.where(
        (eight == 1) & (along == 0), COURANT, jnp.where((eight == 3) & (along == rows - 1), -COURANT, 0.0)
    )
    left = thirds(onto)
    right = thirds(jnp.concatenate([heights, sides], axis=1))
    pairs = [(i, j) for i in range(3) for j in range(3 - i)]
    both = dot(
        jnp.concatenate([left[i] for i, _ in pairs], axis=0).astype(BF16),
        jnp.concatenate([right[j] for _, j in pairs], axis=0).astype(BF16),
        (0, 0),
        None,
    )
    height_ref[...] = solved_ref[...] + wet * both[:, :rows]
    meridional_ref[...] = meridional_part_ref[...] + wet * both[:, rows:]


def call(kernel, outs, in_specs, scratch=()):
    return pl.pallas_call(
        kernel,
        out_shape=outs,
        in_specs=in_specs,
        out_specs=[VMEM] * len(outs),
        scratch_shapes=list(scratch),
        compiler_params=pltpu.CompilerParams(vmem_limit_bytes=LIMIT),
    )


def loading(read):
    return [pltpu.VMEM(x.shape, x.dtype) for x in read], pltpu.SemaphoreType.DMA((len(read),))


def kept(*shape):
    return pltpu.VMEM(shape, F32)


def per_device(
    height_old,
    height_now,
    zonal_old,
    zonal_now,
    meridional_old,
    meridional_now,
    ocean_depth,
    land_sea,
    metric_factor,
    coriolis,
    implicit_weight,
    source_longitude,
    source_latitude,
    source_amplitude,
):
    columns, rows = height_now.shape
    around = lax.axis_size("lon")
    blocks = lax.axis_size("lat")

    def pinned(values):
        return pltpu.with_memory_space_constraint(values, pltpu.HBM)

    height_now, zonal_now, ocean_depth, land_sea, meridional_now, metric = (
        pinned(x) for x in (height_now, zonal_now, ocean_depth, land_sea, meridional_now, metric_factor[None, :])
    )
    read = (
        pinned(implicit_weight.reshape(blocks, rows)),
        height_now,
        zonal_now,
        ocean_depth,
        land_sea,
        pinned(source_longitude.reshape(-1, rows)),
        pinned(source_latitude.reshape(-1, rows)),
        pinned(source_amplitude.reshape(-1, rows)),
        meridional_now,
        pinned(height_old),
        metric,
    )
    held, arrived = loading(read)
    own, to_inner, to_outer, interim, vectors, alpha, beta = call(
        sums_kernel,
        [kept(4, columns), kept(4, columns), kept(4, columns), kept(columns, rows)]
        + [kept(8, rows), kept(blocks, rows), kept(blocks, rows)],
        [HBM] * len(read),
        [*held, pltpu.VMEM((8, blocks, rows), F32), arrived],
    )(*read)

    pairs = [[i, i + 1] for i in range(0, around, 2)]
    inner = lax.all_gather(to_inner, "lon", axis=0, axis_index_groups=pairs)

    groups = [
        [lon * blocks + lat for lon in (first, (first + 1) % around) for lat in range(blocks)]
        for first in range(1, around, 2)
    ]
    (send,) = call(pack_kernel, [kept(2 * blocks, 2, columns)], [VMEM] * 3)(own, inner, to_outer)
    received = lax.all_to_all(send, ("lon", "lat"), 0, 0, axis_index_groups=groups, tiled=True)

    read = (
        height_now,
        zonal_now,
        ocean_depth,
        land_sea,
        meridional_now,
        metric,
        pinned(coriolis[None, :]),
        pinned(zonal_old),
        pinned(meridional_old),
    )
    held, arrived = loading(read)
    wet, zonal_part, meridional_part, green, solved, take, outer = call(
        local_kernel,
        [kept(columns, rows)] * 3
        + [pltpu.VMEM((3, rows, rows), BF16), kept(columns, rows), kept(blocks, 4, rows), kept(1, rows)],
        [HBM] * len(read) + [VMEM] * 4,
        [*held, arrived],
    )(*read, interim, vectors, alpha, beta)

    block = jax.ShapeDtypeStruct((columns, rows), F32)
    return tuple(
        call(finish_kernel, [block] * 3, [VMEM] * 10)(
            received, inner, outer, vectors, green, wet, zonal_part, meridional_part, solved, take
        )
    )


def solution(mesh):
    grid = P("lon", "lat")
    placed = (grid,) * 8 + (P("lat"), P("lat"), P(), P(), P(), P())
    return jax.shard_map(
        per_device, mesh=mesh, in_specs=placed, out_specs=(grid, grid, grid), check_vma=False
    )
```

```python
import jax
import jax.numpy as jnp
from jax import lax
from jax.experimental import pallas as pl
from jax.experimental.pallas import tpu as pltpu
from jax.sharding import PartitionSpec as P

COURANT = 0.25
F32 = jnp.float32
BF16 = jnp.bfloat16
HIGH = lax.Precision.HIGHEST
VMEM = pl.BlockSpec(memory_space=pltpu.VMEM)
HBM = pl.BlockSpec(memory_space=pltpu.HBM)
LIMIT = 8 << 20


def iota(shape, dim):
    return lax.broadcasted_iota(jnp.int32, shape, dim)


def dot(a, b, contract, precision=HIGH):
    return lax.dot_general(
        a, b, ((contract[:1], contract[1:]), ((), ())), precision=precision, preferred_element_type=F32
    )


def matmul2(x, y):
    a, b, c, d = x
    e, f, g, h = y
    return a * e + b * g, a * f + b * h, c * e + d * g, c * f + d * h


def product_scan(mats, axis, direction, rescale):
    shape = mats[0].shape
    size = shape[axis]
    place = iota(shape, axis)
    identity = (1.0, 0.0, 0.0, 1.0)
    step = 1
    while step < size:
        reach = [step * i for i in range(1, min(4, size // step))]
        others = []
        for distance in reach:
            if direction == 1:
                keep, shift = place >= distance, distance
            else:
                keep, shift = place < size - distance, size - distance
            others.append([jnp.where(keep, pltpu.roll(m, shift, axis), i) for m, i in zip(mats, identity)])
        factors = [mats, *others]
        while len(factors) > 1:
            factors = [matmul2(x, y) for x, y in zip(factors[::2], factors[1::2])]
        mats = factors[0]
        if rescale:
            factor = 1.0 / (mats[0] + mats[1] + mats[2] + mats[3])
            mats = tuple(m * factor for m in mats)
        step *= len(reach) + 1
    return mats


def lane(values, index):
    return jnp.broadcast_to(values[:, index : index + 1], values.shape)


def running_product(values, direction):
    size = values.shape[0]
    row = iota(values.shape, 0)
    step = 1
    while step < size:
        if direction == 1:
            keep, shift = row >= step, step
        else:
            keep, shift = row < size - step, size - step
        values = values * jnp.where(keep, pltpu.roll(values, shift, 0), 1.0)
        step *= 2
    return values


def differences(values, axis):
    size = values.shape[axis]
    place = iota(values.shape, axis)
    after = jnp.where(place == size - 1, 0.0, pltpu.roll(values, size - 1, axis))
    before = jnp.where(place == 0, 0.0, pltpu.roll(values, 1, axis))
    return after - before


def load(sources, held, arrived):
    copies = [pltpu.make_async_copy(src, dst, arrived.at[i]) for i, (src, dst) in enumerate(zip(sources, held))]
    for copy in copies:
        copy.start()
    return copies


def select_rows(row, parts):
    out = jnp.zeros(row.shape, F32)
    for index, part in enumerate(parts):
        out = jnp.where(row == index, part, out)
    return out


def thirds(values):
    high = values.astype(BF16).astype(F32)
    rest = values - high
    middle = rest.astype(BF16).astype(F32)
    return high, middle, rest - middle


def sums_dot(a, b):
    size = a.shape[0]
    left = jnp.concatenate(thirds(a), axis=0).astype(BF16)
    out = jnp.zeros((size, b.shape[0]), F32)
    for skip, part in enumerate(thirds(b)):
        product = dot(left, part.astype(BF16), (1, 1), None)
        for index in range(3 - skip):
            out += product[index * size : (index + 1) * size]
    return out


def sums_kernel(*refs):
    count = 11
    sources, refs = refs[:count], refs[count:]
    (own_ref, to_inner_ref, to_outer_ref, interim_ref, vectors_ref, alpha_ref, beta_ref), refs = refs[:7], refs[7:]
    held, rows_ref, arrived = refs[:count], refs[count], refs[count + 1]
    copies = load(sources, held, arrived)
    (
        weight_ref,
        height_now_ref,
        zonal_ref,
        depth_ref,
        land_ref,
        lon_ref,
        lat_ref,
        amount_ref,
        meridional_ref,
        height_old_ref,
        metric_ref,
    ) = held
    columns, rows = height_now_ref.shape
    blocks = weight_ref.shape[0]
    block = lax.axis_index("lat")
    first_east = lax.axis_index("lon") * columns
    first_north = block * rows

    for copy in copies:
        copy.wait()
    c = 1.0 / weight_ref[...]
    one = jnp.ones_like(c)
    mats = (1.0 + c, one, c, one)
    up = product_scan(mats, 1, 1, False)
    down = product_scan(mats, 1, -1, False)
    up_all = tuple(lane(m, rows - 1) for m in up)
    down_all = tuple(lane(m, 0) for m in down)
    factor = 1.0 / (up_all[0] + up_all[1] + up_all[2] + up_all[3])
    ahead = product_scan(tuple(m * factor for m in up_all), 0, 1, True)
    factor = 1.0 / (down_all[0] + down_all[1] + down_all[2] + down_all[3])
    behind = product_scan(tuple(m * factor for m in down_all), 0, -1, True)
    row = iota(c.shape, 0)
    place = iota(c.shape, 1)
    rho = jnp.where(
        row == 0, 1.0, pltpu.roll((ahead[2] + ahead[3]) / (ahead[0] + ahead[1]), 1, 0)
    )
    sigma = jnp.where(
        row == blocks - 1,
        1.0,
        pltpu.roll((behind[2] + behind[3]) / (behind[0] + behind[1]), blocks - 1, 0),
    )
    p_after = up[0] + up[1] * rho
    q_before = down[0] + down[1] * sigma
    p = jnp.where(place == 0, 1.0, pltpu.roll(p_after, 1, 1))
    q = jnp.where(place == rows - 1, 1.0, pltpu.roll(q_before, rows - 1, 1))
    p_end = up_all[0] + up_all[1] * rho
    q_end = down_all[0] + down_all[1] * sigma
    scale = 1.0 / (up_all[2] + up_all[3] * rho + lane(p, rows - 1) * sigma)
    c_below = jnp.where(row == 0, 0.0, pltpu.roll(lane(c, rows - 1), 1, 0))
    c_above = jnp.where(row == blocks - 1, 0.0, pltpu.roll(lane(c, 0), blocks - 1, 0))
    low_p = -COURANT * c_below * (1.0 - rho)
    low_q = -COURANT * c_below * q_end
    high_p = COURANT * c_above * p_end
    high_q = COURANT * c_above * (1.0 - sigma)
    stacked = (
        p * c,
        q * c,
        q * scale,
        p * scale,
        low_p * q * scale,
        high_q * p * scale,
        jnp.where(place == 0, low_p, jnp.where(place == rows - 1, high_p, 0.0)),
        jnp.where(place == 0, low_q, jnp.where(place == rows - 1, high_q, 0.0)),
    )
    alpha_ref[...] = 1.0 / p_end
    beta_ref[...] = 1.0 / q_end
    for index, values in enumerate(stacked):
        rows_ref[index] = values
        vectors_ref[index : index + 1, :] = rows_ref[index, pl.ds(block, 1), :]

    shape = (columns, rows)
    subs = iota(shape, 0)
    added = jnp.zeros(shape, F32)
    parts = thirds(amount_ref[...])
    chunks = range(lon_ref.shape[0])
    here = [lon_ref[i : i + 1, :] - first_east == subs for i in chunks]
    there = jnp.concatenate(
        [jnp.where(lat_ref[i : i + 1, :] - first_north == subs, 1.0, 0.0) for i in chunks], axis=1
    ).astype(BF16)
    for part in parts:
        amounts = jnp.concatenate([jnp.where(here[i], part[i : i + 1, :], 0.0) for i in chunks], axis=1)
        added += dot(amounts.astype(BF16), there, (1, 1), None)

    depth = depth_ref[...] * land_ref[...].astype(F32)
    flux_east = depth * zonal_ref[...]
    flux_north = depth * meridional_ref[...]
    metric = metric_ref[...]
    interim = (
        height_old_ref[...]
        - COURANT * (metric * differences(flux_east, 0) + differences(flux_north, 1))
        + added
    )
    interim_ref[...] = interim

    eight = iota((8, rows), 0)
    along = iota((8, rows), 1)
    vectors = vectors_ref[...]
    on_interim = jnp.where(eight < 2, vectors, 0.0)
    on_edges = jnp.where(eight < 2, pltpu.roll(vectors, 2, 0), 0.0)
    on_edges += jnp.where((eight == 2) & (along == 1) | (eight == 3) & (along == 2), 1.0, 0.0)
    lanes = iota(shape, 1)
    edges = jnp.where((lanes == 0) | (lanes == rows - 1), flux_north, pltpu.roll(height_now_ref[...], 2, 1))
    total = sums_dot(
        jnp.concatenate([on_interim, on_edges], axis=1), jnp.concatenate([interim, edges], axis=1)
    )
    own_ref[...] = total[0:4]

    last = columns - 1
    odd = jnp.full((8, columns), lax.axis_index("lon") & 1, jnp.int32) == 1
    line = iota((8, columns), 1)
    onto = COURANT * metric * vectors
    flux_first, flux_last = flux_east[0:1, :], flux_east[last:columns, :]
    to_west = jnp.where(line == last, -jnp.sum(onto * flux_first, axis=1, keepdims=True), 0.0)
    to_east = jnp.where(line == 0, jnp.sum(onto * flux_last, axis=1, keepdims=True), 0.0)
    to_west = jnp.where(eight < 2, to_west, jnp.where(eight == 2, height_now_ref[0:1, :], flux_first))
    to_east = jnp.where(eight < 2, to_east, jnp.where(eight == 2, height_now_ref[last:columns, :], flux_last))
    to_inner_ref[...] = jnp.where(odd, to_west, to_east)[0:4]
    to_outer_ref[...] = jnp.where(odd, to_east, to_west)[0:4]


def pack_kernel(own_ref, inner_ref, to_outer_ref, send_ref):
    blocks = send_ref.shape[0] // 2
    block = lax.axis_index("lat")
    parity = lax.axis_index("lon") & 1
    at_own, at_outer = parity * blocks, (1 - parity) * blocks
    own = own_ref[...]
    row = iota(own.shape, 0)
    own += jnp.where(row < 2, inner_ref[1 - parity], 0.0)
    outer = to_outer_ref[...]
    own_up = jnp.concatenate([own[0:1], own[2:3]], axis=0)
    own_down = jnp.concatenate([own[1:2], own[3:4]], axis=0)
    outer_up = jnp.concatenate([outer[0:1], jnp.zeros_like(outer[0:1])], axis=0)
    outer_down = jnp.concatenate([outer[1:2], jnp.zeros_like(outer[0:1])], axis=0)
    for target in range(blocks):
        north = jnp.full(own_up.shape, (block < target).astype(jnp.int32), jnp.int32) == 1
        slot = blocks - 1 - target
        send_ref[at_own + slot] = jnp.where(north, own_up, own_down)
        send_ref[at_outer + slot] = jnp.where(north, outer_up, outer_down)
    send_ref[at_outer + blocks - 1 - block] = outer[2:4]


def local_kernel(*refs):
    count = 9
    sources, refs = refs[:count], refs[count:]
    (interim_ref, vectors_ref, alpha_ref, beta_ref), refs = refs[:4], refs[4:]
    (wet_ref, zonal_part_ref, meridional_part_ref, green_ref, solved_ref, take_ref, outer_ref), refs = refs[:7], refs[7:]
    held, arrived = refs[:count], refs[count]
    copies = load(sources, held, arrived)
    (
        height_now_ref,
        zonal_ref,
        depth_ref,
        land_ref,
        meridional_ref,
        metric_ref,
        coriolis_ref,
        zonal_old_ref,
        meridional_old_ref,
    ) = held
    shape = height_now_ref.shape
    rows = shape[1]
    subs = iota(shape, 0)
    lanes = iota(shape, 1)
    blocks = alpha_ref.shape[0]
    block = lax.axis_index("lat")

    row = iota(alpha_ref.shape, 0)
    from_south = running_product(jnp.where(row < block, alpha_ref[...], 1.0), -1)
    from_north = running_product(jnp.where(row > block, beta_ref[...], 1.0), 1)
    weights = (
        jnp.where(row < block, from_south, 0.0),
        jnp.where(row == block - 1, 1.0, 0.0),
        jnp.where(row > block, from_north, 0.0),
        jnp.where(row == block + 1, 1.0, 0.0),
    )
    for source in range(blocks):
        for index, values in enumerate(weights):
            take_ref[source, index : index + 1, :] = values[source : source + 1, :]

    for copy in copies:
        copy.wait()
    wet = land_ref[...].astype(F32)
    flux_north = depth_ref[...] * wet * meridional_ref[...]

    vectors = vectors_ref[...]
    p_from = jnp.broadcast_to(vectors[0:1, :], shape).T
    q_from = jnp.broadcast_to(vectors[1:2, :], shape).T
    green = jnp.where(subs <= lanes, p_from * vectors[2:3, :], q_from * vectors[3:4, :])
    for index, part in enumerate(thirds(green)):
        green_ref[index] = part.astype(BF16)
    solved = dot(interim_ref[...], green, (1, 0))
    solved += flux_north[:, 0:1] * vectors[4:5, :] + flux_north[:, rows - 1 : rows] * vectors[5:6, :]
    solved_ref[...] = wet * solved

    height = height_now_ref[...]
    outer_ref[...] = COURANT * metric_ref[...]
    turning = coriolis_ref[...]
    wet_ref[...] = wet
    zonal_part_ref[...] = wet * (
        zonal_old_ref[...] - COURANT * metric_ref[...] * differences(height, 0) + turning * meridional_ref[...]
    )
    meridional_part_ref[...] = wet * (
        meridional_old_ref[...] - COURANT * differences(height, 1) - turning * zonal_ref[...]
    )


def finish_kernel(
    received_ref,
    inner_ref,
    outer_ref,
    vectors_ref,
    green_ref,
    wet_ref,
    zonal_part_ref,
    meridional_part_ref,
    solved_ref,
    take_ref,
    height_ref,
    zonal_ref,
    meridional_ref,
):
    columns, rows = wet_ref.shape
    blocks = take_ref.shape[0]
    last = columns - 1
    wet = wet_ref[...]
    outer = outer_ref[...]
    eight = iota((8, rows), 0)
    along = iota((8, columns), 1)
    block = lax.axis_index("lat")
    parity = lax.axis_index("lon") & 1
    at_own, at_other = parity * blocks, (1 - parity) * blocks

    inner = inner_ref[1 - parity][2:4]
    other = received_ref[at_other + blocks - 1 - block]
    odd = jnp.full(other.shape, parity, jnp.int32) == 1
    west = jnp.where(odd, inner, other)
    east = jnp.where(odd, other, inner)
    zonal_ref[...] = zonal_part_ref[...]
    zonal_ref[0:1, :] += wet_ref[0:1, :] * outer * west[0:1, :]
    zonal_ref[last:columns, :] -= wet_ref[last:columns, :] * outer * east[0:1, :]

    halo = select_rows(eight, (0.0, 0.0, 0.0, 0.0, outer * west[1:2, :], -outer * east[1:2, :]))
    left = jnp.concatenate(thirds(halo), axis=0).astype(BF16)
    outer_rows = jnp.zeros((8, rows), F32)
    for skip in range(3):
        product = dot(left, green_ref[skip], (1, 0), None)
        for index in range(3 - skip):
            outer_rows += product[8 * index : 8 * index + 8]

    south = jnp.zeros(other.shape, F32)
    north = jnp.zeros(other.shape, F32)
    for source in range(blocks):
        slot = blocks - 1 - source
        values = received_ref[at_own + slot] + received_ref[at_other + slot]
        take = take_ref[source]
        south += take[0:2] * values
        north += take[2:4] * values
    onto = jnp.concatenate([south, north, jnp.zeros((4, columns), F32)], axis=0)
    onto = jnp.where((eight == 4) & (along == 0) | (eight == 5) & (along == last), 1.0, onto)
    heights = select_rows(
        eight, (vectors_ref[2:3, :], 0.0, vectors_ref[3:4, :], 0.0, outer_rows, outer_rows)
    )
    sides = jnp.where(
        (eight == 1) & (along == 0), COURANT, jnp.where((eight == 3) & (along == rows - 1), -COURANT, 0.0)
    )
    left = thirds(onto)
    right = thirds(jnp.concatenate([heights, sides], axis=1))
    pairs = [(i, j) for i in range(3) for j in range(3 - i)]
    both = dot(
        jnp.concatenate([left[i] for i, _ in pairs], axis=0).astype(BF16),
        jnp.concatenate([right[j] for _, j in pairs], axis=0).astype(BF16),
        (0, 0),
        None,
    )
    height_ref[...] = solved_ref[...] + wet * both[:, :rows]
    meridional_ref[...] = meridional_part_ref[...] + wet * both[:, rows:]


def call(kernel, outs, in_specs, scratch=()):
    return pl.pallas_call(
        kernel,
        out_shape=outs,
        in_specs=in_specs,
        out_specs=[VMEM] * len(outs),
        scratch_shapes=list(scratch),
        compiler_params=pltpu.CompilerParams(vmem_limit_bytes=LIMIT),
    )


def loading(read):
    return [pltpu.VMEM(x.shape, x.dtype) for x in read], pltpu.SemaphoreType.DMA((len(read),))


def kept(*shape):
    return pltpu.VMEM(shape, F32)


def per_device(
    height_old,
    height_now,
    zonal_old,
    zonal_now,
    meridional_old,
    meridional_now,
    ocean_depth,
    land_sea,
    metric_factor,
    coriolis,
    implicit_weight,
    source_longitude,
    source_latitude,
    source_amplitude,
):
    columns, rows = height_now.shape
    around = lax.axis_size("lon")
    blocks = lax.axis_size("lat")

    def pinned(values):
        return pltpu.with_memory_space_constraint(values, pltpu.HBM)

    height_now, zonal_now, ocean_depth, land_sea, meridional_now, metric = (
        pinned(x) for x in (height_now, zonal_now, ocean_depth, land_sea, meridional_now, metric_factor[None, :])
    )
    read = (
        pinned(implicit_weight.reshape(blocks, rows)),
        height_now,
        zonal_now,
        ocean_depth,
        land_sea,
        pinned(source_longitude.reshape(-1, rows)),
        pinned(source_latitude.reshape(-1, rows)),
        pinned(source_amplitude.reshape(-1, rows)),
        meridional_now,
        pinned(height_old),
        metric,
    )
    held, arrived = loading(read)
    own, to_inner, to_outer, interim, vectors, alpha, beta = call(
        sums_kernel,
        [kept(4, columns), kept(4, columns), kept(4, columns), kept(columns, rows)]
        + [kept(8, rows), kept(blocks, rows), kept(blocks, rows)],
        [HBM] * len(read),
        [*held, pltpu.VMEM((8, blocks, rows), F32), arrived],
    )(*read)

    pairs = [[i, i + 1] for i in range(0, around, 2)]
    inner = lax.all_gather(to_inner, "lon", axis=0, axis_index_groups=pairs)

    groups = [
        [lon * blocks + lat for lon in ((first + 1) % around, first) for lat in reversed(range(blocks))]
        for first in range(1, around, 2)
    ]
    (send,) = call(pack_kernel, [kept(2 * blocks, 2, columns)], [VMEM] * 3)(own, inner, to_outer)
    received = lax.all_to_all(send, ("lon", "lat"), 0, 0, axis_index_groups=groups, tiled=True)

    read = (
        height_now,
        zonal_now,
        ocean_depth,
        land_sea,
        meridional_now,
        metric,
        pinned(coriolis[None, :]),
        pinned(zonal_old),
        pinned(meridional_old),
    )
    held, arrived = loading(read)
    wet, zonal_part, meridional_part, green, solved, take, outer = call(
        local_kernel,
        [kept(columns, rows)] * 3
        + [pltpu.VMEM((3, rows, rows), BF16), kept(columns, rows), kept(blocks, 4, rows), kept(1, rows)],
        [HBM] * len(read) + [VMEM] * 4,
        [*held, arrived],
    )(*read, interim, vectors, alpha, beta)

    block = jax.ShapeDtypeStruct((columns, rows), F32)
    return tuple(
        call(finish_kernel, [block] * 3, [VMEM] * 10)(
            received, inner, outer, vectors, green, wet, zonal_part, meridional_part, solved, take
        )
    )


def solution(mesh):
    grid = P("lon", "lat")
    placed = (grid,) * 8 + (P("lat"), P("lat"), P(), P(), P(), P())
    return jax.shard_map(
        per_device, mesh=mesh, in_specs=placed, out_specs=(grid, grid, grid), check_vma=False
    )
```

```python
import jax
import jax.numpy as jnp
from jax import lax
from jax.experimental import pallas as pl
from jax.experimental.pallas import tpu as pltpu
from jax.sharding import PartitionSpec as P

COURANT = 0.25
F32 = jnp.float32
BF16 = jnp.bfloat16
HIGH = lax.Precision.HIGHEST
VMEM = pl.BlockSpec(memory_space=pltpu.VMEM)
HBM = pl.BlockSpec(memory_space=pltpu.HBM)
LIMIT = 8 << 20


def iota(shape, dim):
    return lax.broadcasted_iota(jnp.int32, shape, dim)


def dot(a, b, contract, precision=HIGH):
    return lax.dot_general(
        a, b, ((contract[:1], contract[1:]), ((), ())), precision=precision, preferred_element_type=F32
    )


def matmul2(x, y):
    a, b, c, d = x
    e, f, g, h = y
    return a * e + b * g, a * f + b * h, c * e + d * g, c * f + d * h


def product_scan(mats, axis, direction, rescale):
    shape = mats[0].shape
    size = shape[axis]
    place = iota(shape, axis)
    identity = (1.0, 0.0, 0.0, 1.0)
    step = 1
    while step < size:
        reach = [step * i for i in range(1, min(4, size // step))]
        others = []
        for distance in reach:
            if direction == 1:
                keep, shift = place >= distance, distance
            else:
                keep, shift = place < size - distance, size - distance
            others.append([jnp.where(keep, pltpu.roll(m, shift, axis), i) for m, i in zip(mats, identity)])
        factors = [mats, *others]
        while len(factors) > 1:
            factors = [matmul2(x, y) for x, y in zip(factors[::2], factors[1::2])]
        mats = factors[0]
        if rescale:
            factor = 1.0 / (mats[0] + mats[1] + mats[2] + mats[3])
            mats = tuple(m * factor for m in mats)
        step *= len(reach) + 1
    return mats


def lane(values, index):
    return jnp.broadcast_to(values[:, index : index + 1], values.shape)


def running_product(values, direction):
    size = values.shape[0]
    row = iota(values.shape, 0)
    step = 1
    while step < size:
        if direction == 1:
            keep, shift = row >= step, step
        else:
            keep, shift = row < size - step, size - step
        values = values * jnp.where(keep, pltpu.roll(values, shift, 0), 1.0)
        step *= 2
    return values


def differences(values, axis):
    size = values.shape[axis]
    place = iota(values.shape, axis)
    after = jnp.where(place == size - 1, 0.0, pltpu.roll(values, size - 1, axis))
    before = jnp.where(place == 0, 0.0, pltpu.roll(values, 1, axis))
    return after - before


def place(lat, blocks):
    half = blocks // 2
    if isinstance(lat, int):
        return blocks - 1 - lat if lat >= half else half + lat
    return jnp.where(lat >= half, blocks - 1 - lat, half + lat)


def load(sources, held, arrived):
    copies = [pltpu.make_async_copy(src, dst, arrived.at[i]) for i, (src, dst) in enumerate(zip(sources, held))]
    for copy in copies:
        copy.start()
    return copies


def select_rows(row, parts):
    out = jnp.zeros(row.shape, F32)
    for index, part in enumerate(parts):
        out = jnp.where(row == index, part, out)
    return out


def thirds(values):
    high = values.astype(BF16).astype(F32)
    rest = values - high
    middle = rest.astype(BF16).astype(F32)
    return high, middle, rest - middle


def sums_dot(a, b):
    size = a.shape[0]
    left = jnp.concatenate(thirds(a), axis=0).astype(BF16)
    out = jnp.zeros((size, b.shape[0]), F32)
    for skip, part in enumerate(thirds(b)):
        product = dot(left, part.astype(BF16), (1, 1), None)
        for index in range(3 - skip):
            out += product[index * size : (index + 1) * size]
    return out


def sums_kernel(*refs):
    count = 11
    sources, refs = refs[:count], refs[count:]
    (own_ref, to_inner_ref, to_outer_ref, interim_ref, vectors_ref, alpha_ref, beta_ref), refs = refs[:7], refs[7:]
    held, rows_ref, arrived = refs[:count], refs[count], refs[count + 1]
    copies = load(sources, held, arrived)
    (
        weight_ref,
        height_now_ref,
        zonal_ref,
        depth_ref,
        land_ref,
        lon_ref,
        lat_ref,
        amount_ref,
        meridional_ref,
        height_old_ref,
        metric_ref,
    ) = held
    columns, rows = height_now_ref.shape
    blocks = weight_ref.shape[0]
    block = lax.axis_index("lat")
    first_east = lax.axis_index("lon") * columns
    first_north = block * rows

    for copy in copies:
        copy.wait()
    c = 1.0 / weight_ref[...]
    one = jnp.ones_like(c)
    mats = (1.0 + c, one, c, one)
    up = product_scan(mats, 1, 1, False)
    down = product_scan(mats, 1, -1, False)
    up_all = tuple(lane(m, rows - 1) for m in up)
    down_all = tuple(lane(m, 0) for m in down)
    factor = 1.0 / (up_all[0] + up_all[1] + up_all[2] + up_all[3])
    ahead = product_scan(tuple(m * factor for m in up_all), 0, 1, True)
    factor = 1.0 / (down_all[0] + down_all[1] + down_all[2] + down_all[3])
    behind = product_scan(tuple(m * factor for m in down_all), 0, -1, True)
    row = iota(c.shape, 0)
    place = iota(c.shape, 1)
    rho = jnp.where(
        row == 0, 1.0, pltpu.roll((ahead[2] + ahead[3]) / (ahead[0] + ahead[1]), 1, 0)
    )
    sigma = jnp.where(
        row == blocks - 1,
        1.0,
        pltpu.roll((behind[2] + behind[3]) / (behind[0] + behind[1]), blocks - 1, 0),
    )
    p_after = up[0] + up[1] * rho
    q_before = down[0] + down[1] * sigma
    p = jnp.where(place == 0, 1.0, pltpu.roll(p_after, 1, 1))
    q = jnp.where(place == rows - 1, 1.0, pltpu.roll(q_before, rows - 1, 1))
    p_end = up_all[0] + up_all[1] * rho
    q_end = down_all[0] + down_all[1] * sigma
    scale = 1.0 / (up_all[2] + up_all[3] * rho + lane(p, rows - 1) * sigma)
    c_below = jnp.where(row == 0, 0.0, pltpu.roll(lane(c, rows - 1), 1, 0))
    c_above = jnp.where(row == blocks - 1, 0.0, pltpu.roll(lane(c, 0), blocks - 1, 0))
    low_p = -COURANT * c_below * (1.0 - rho)
    low_q = -COURANT * c_below * q_end
    high_p = COURANT * c_above * p_end
    high_q = COURANT * c_above * (1.0 - sigma)
    stacked = (
        p * c,
        q * c,
        q * scale,
        p * scale,
        low_p * q * scale,
        high_q * p * scale,
        jnp.where(place == 0, low_p, jnp.where(place == rows - 1, high_p, 0.0)),
        jnp.where(place == 0, low_q, jnp.where(place == rows - 1, high_q, 0.0)),
    )
    alpha_ref[...] = 1.0 / p_end
    beta_ref[...] = 1.0 / q_end
    for index, values in enumerate(stacked):
        rows_ref[index] = values
        vectors_ref[index : index + 1, :] = rows_ref[index, pl.ds(block, 1), :]

    shape = (columns, rows)
    subs = iota(shape, 0)
    added = jnp.zeros(shape, F32)
    parts = thirds(amount_ref[...])
    chunks = range(lon_ref.shape[0])
    here = [lon_ref[i : i + 1, :] - first_east == subs for i in chunks]
    there = jnp.concatenate(
        [jnp.where(lat_ref[i : i + 1, :] - first_north == subs, 1.0, 0.0) for i in chunks], axis=1
    ).astype(BF16)
    for part in parts:
        amounts = jnp.concatenate([jnp.where(here[i], part[i : i + 1, :], 0.0) for i in chunks], axis=1)
        added += dot(amounts.astype(BF16), there, (1, 1), None)

    depth = depth_ref[...] * land_ref[...].astype(F32)
    flux_east = depth * zonal_ref[...]
    flux_north = depth * meridional_ref[...]
    metric = metric_ref[...]
    interim = (
        height_old_ref[...]
        - COURANT * (metric * differences(flux_east, 0) + differences(flux_north, 1))
        + added
    )
    interim_ref[...] = interim

    eight = iota((8, rows), 0)
    along = iota((8, rows), 1)
    vectors = vectors_ref[...]
    on_interim = jnp.where(eight < 2, vectors, 0.0)
    on_edges = jnp.where(eight < 2, pltpu.roll(vectors, 2, 0), 0.0)
    on_edges += jnp.where((eight == 2) & (along == 1) | (eight == 3) & (along == 2), 1.0, 0.0)
    lanes = iota(shape, 1)
    edges = jnp.where((lanes == 0) | (lanes == rows - 1), flux_north, pltpu.roll(height_now_ref[...], 2, 1))
    total = sums_dot(
        jnp.concatenate([on_interim, on_edges], axis=1), jnp.concatenate([interim, edges], axis=1)
    )
    own_ref[...] = total[0:4]

    last = columns - 1
    odd = jnp.full((8, columns), lax.axis_index("lon") & 1, jnp.int32) == 1
    line = iota((8, columns), 1)
    onto = COURANT * metric * vectors
    flux_first, flux_last = flux_east[0:1, :], flux_east[last:columns, :]
    to_west = jnp.where(line == last, -jnp.sum(onto * flux_first, axis=1, keepdims=True), 0.0)
    to_east = jnp.where(line == 0, jnp.sum(onto * flux_last, axis=1, keepdims=True), 0.0)
    to_west = jnp.where(eight < 2, to_west, jnp.where(eight == 2, height_now_ref[0:1, :], flux_first))
    to_east = jnp.where(eight < 2, to_east, jnp.where(eight == 2, height_now_ref[last:columns, :], flux_last))
    to_inner_ref[...] = jnp.where(odd, to_west, to_east)[0:4]
    to_outer_ref[...] = jnp.where(odd, to_east, to_west)[0:4]


def pack_kernel(own_ref, inner_ref, to_outer_ref, send_ref):
    blocks = send_ref.shape[0] // 2
    block = lax.axis_index("lat")
    parity = lax.axis_index("lon") & 1
    own = own_ref[...]
    row = iota(own.shape, 0)
    own += jnp.where(row < 2, inner_ref[1 - parity], 0.0)
    outer = to_outer_ref[...]
    own_up = jnp.concatenate([own[0:1], own[2:3]], axis=0)
    own_down = jnp.concatenate([own[1:2], own[3:4]], axis=0)
    outer_up = jnp.concatenate([outer[0:1], jnp.zeros_like(outer[0:1])], axis=0)
    outer_down = jnp.concatenate([outer[1:2], jnp.zeros_like(outer[0:1])], axis=0)
    for target in range(blocks):
        north = jnp.full(own_up.shape, (block < target).astype(jnp.int32), jnp.int32) == 1
        slot = 2 * place(target, blocks)
        send_ref[slot + parity] = jnp.where(north, own_up, own_down)
        send_ref[slot + 1 - parity] = jnp.where(north, outer_up, outer_down)
    send_ref[2 * place(block, blocks) + 1 - parity] = outer[2:4]


def local_kernel(*refs):
    count = 9
    sources, refs = refs[:count], refs[count:]
    (interim_ref, vectors_ref, alpha_ref, beta_ref), refs = refs[:4], refs[4:]
    (wet_ref, zonal_part_ref, meridional_part_ref, green_ref, solved_ref, take_ref, outer_ref), refs = refs[:7], refs[7:]
    held, arrived = refs[:count], refs[count]
    copies = load(sources, held, arrived)
    (
        height_now_ref,
        zonal_ref,
        depth_ref,
        land_ref,
        meridional_ref,
        metric_ref,
        coriolis_ref,
        zonal_old_ref,
        meridional_old_ref,
    ) = held
    shape = height_now_ref.shape
    rows = shape[1]
    subs = iota(shape, 0)
    lanes = iota(shape, 1)
    blocks = alpha_ref.shape[0]
    block = lax.axis_index("lat")

    row = iota(alpha_ref.shape, 0)
    from_south = running_product(jnp.where(row < block, alpha_ref[...], 1.0), -1)
    from_north = running_product(jnp.where(row > block, beta_ref[...], 1.0), 1)
    weights = (
        jnp.where(row < block, from_south, 0.0),
        jnp.where(row == block - 1, 1.0, 0.0),
        jnp.where(row > block, from_north, 0.0),
        jnp.where(row == block + 1, 1.0, 0.0),
    )
    for source in range(blocks):
        for index, values in enumerate(weights):
            take_ref[source, index : index + 1, :] = values[source : source + 1, :]

    for copy in copies:
        copy.wait()
    wet = land_ref[...].astype(F32)
    flux_north = depth_ref[...] * wet * meridional_ref[...]

    vectors = vectors_ref[...]
    p_from = jnp.broadcast_to(vectors[0:1, :], shape).T
    q_from = jnp.broadcast_to(vectors[1:2, :], shape).T
    green = jnp.where(subs <= lanes, p_from * vectors[2:3, :], q_from * vectors[3:4, :])
    for index, part in enumerate(thirds(green)):
        green_ref[index] = part.astype(BF16)
    solved = dot(interim_ref[...], green, (1, 0))
    solved += flux_north[:, 0:1] * vectors[4:5, :] + flux_north[:, rows - 1 : rows] * vectors[5:6, :]
    solved_ref[...] = wet * solved

    height = height_now_ref[...]
    outer_ref[...] = COURANT * metric_ref[...]
    turning = coriolis_ref[...]
    wet_ref[...] = wet
    zonal_part_ref[...] = wet * (
        zonal_old_ref[...] - COURANT * metric_ref[...] * differences(height, 0) + turning * meridional_ref[...]
    )
    meridional_part_ref[...] = wet * (
        meridional_old_ref[...] - COURANT * differences(height, 1) - turning * zonal_ref[...]
    )


def finish_kernel(
    received_ref,
    inner_ref,
    outer_ref,
    vectors_ref,
    green_ref,
    wet_ref,
    zonal_part_ref,
    meridional_part_ref,
    solved_ref,
    take_ref,
    height_ref,
    zonal_ref,
    meridional_ref,
):
    columns, rows = wet_ref.shape
    blocks = take_ref.shape[0]
    last = columns - 1
    wet = wet_ref[...]
    outer = outer_ref[...]
    eight = iota((8, rows), 0)
    along = iota((8, columns), 1)
    block = lax.axis_index("lat")
    parity = lax.axis_index("lon") & 1

    inner = inner_ref[1 - parity][2:4]
    other = received_ref[2 * place(block, blocks) + 1 - parity]
    odd = jnp.full(other.shape, parity, jnp.int32) == 1
    west = jnp.where(odd, inner, other)
    east = jnp.where(odd, other, inner)
    zonal_ref[...] = zonal_part_ref[...]
    zonal_ref[0:1, :] += wet_ref[0:1, :] * outer * west[0:1, :]
    zonal_ref[last:columns, :] -= wet_ref[last:columns, :] * outer * east[0:1, :]

    halo = select_rows(eight, (0.0, 0.0, 0.0, 0.0, outer * west[1:2, :], -outer * east[1:2, :]))
    left = jnp.concatenate(thirds(halo), axis=0).astype(BF16)
    outer_rows = jnp.zeros((8, rows), F32)
    for skip in range(3):
        product = dot(left, green_ref[skip], (1, 0), None)
        for index in range(3 - skip):
            outer_rows += product[8 * index : 8 * index + 8]

    south = jnp.zeros(other.shape, F32)
    north = jnp.zeros(other.shape, F32)
    for source in range(blocks):
        slot = 2 * place(source, blocks)
        values = received_ref[slot] + received_ref[slot + 1]
        take = take_ref[source]
        south += take[0:2] * values
        north += take[2:4] * values
    onto = jnp.concatenate([south, north, jnp.zeros((4, columns), F32)], axis=0)
    onto = jnp.where((eight == 4) & (along == 0) | (eight == 5) & (along == last), 1.0, onto)
    heights = select_rows(
        eight, (vectors_ref[2:3, :], 0.0, vectors_ref[3:4, :], 0.0, outer_rows, outer_rows)
    )
    sides = jnp.where(
        (eight == 1) & (along == 0), COURANT, jnp.where((eight == 3) & (along == rows - 1), -COURANT, 0.0)
    )
    left = thirds(onto)
    right = thirds(jnp.concatenate([heights, sides], axis=1))
    pairs = [(i, j) for i in range(3) for j in range(3 - i)]
    both = dot(
        jnp.concatenate([left[i] for i, _ in pairs], axis=0).astype(BF16),
        jnp.concatenate([right[j] for _, j in pairs], axis=0).astype(BF16),
        (0, 0),
        None,
    )
    height_ref[...] = solved_ref[...] + wet * both[:, :rows]
    meridional_ref[...] = meridional_part_ref[...] + wet * both[:, rows:]


def call(kernel, outs, in_specs, scratch=()):
    return pl.pallas_call(
        kernel,
        out_shape=outs,
        in_specs=in_specs,
        out_specs=[VMEM] * len(outs),
        scratch_shapes=list(scratch),
        compiler_params=pltpu.CompilerParams(vmem_limit_bytes=LIMIT),
    )


def loading(read):
    return [pltpu.VMEM(x.shape, x.dtype) for x in read], pltpu.SemaphoreType.DMA((len(read),))


def kept(*shape):
    return pltpu.VMEM(shape, F32)


def per_device(
    height_old,
    height_now,
    zonal_old,
    zonal_now,
    meridional_old,
    meridional_now,
    ocean_depth,
    land_sea,
    metric_factor,
    coriolis,
    implicit_weight,
    source_longitude,
    source_latitude,
    source_amplitude,
):
    columns, rows = height_now.shape
    around = lax.axis_size("lon")
    blocks = lax.axis_size("lat")

    def pinned(values):
        return pltpu.with_memory_space_constraint(values, pltpu.HBM)

    height_now, zonal_now, ocean_depth, land_sea, meridional_now, metric = (
        pinned(x) for x in (height_now, zonal_now, ocean_depth, land_sea, meridional_now, metric_factor[None, :])
    )
    read = (
        pinned(implicit_weight.reshape(blocks, rows)),
        height_now,
        zonal_now,
        ocean_depth,
        land_sea,
        pinned(source_longitude.reshape(-1, rows)),
        pinned(source_latitude.reshape(-1, rows)),
        pinned(source_amplitude.reshape(-1, rows)),
        meridional_now,
        pinned(height_old),
        metric,
    )
    held, arrived = loading(read)
    own, to_inner, to_outer, interim, vectors, alpha, beta = call(
        sums_kernel,
        [kept(4, columns), kept(4, columns), kept(4, columns), kept(columns, rows)]
        + [kept(8, rows), kept(blocks, rows), kept(blocks, rows)],
        [HBM] * len(read),
        [*held, pltpu.VMEM((8, blocks, rows), F32), arrived],
    )(*read)

    pairs = [[i, i + 1] for i in range(0, around, 2)]
    inner = lax.all_gather(to_inner, "lon", axis=0, axis_index_groups=pairs)

    order = sorted(range(blocks), key=lambda lat: place(lat, blocks))
    groups = [
        [lon * blocks + lat for lat in order for lon in ((first + 1) % around, first)]
        for first in range(1, around, 2)
    ]
    (send,) = call(pack_kernel, [kept(2 * blocks, 2, columns)], [VMEM] * 3)(own, inner, to_outer)
    received = lax.all_to_all(send, ("lon", "lat"), 0, 0, axis_index_groups=groups, tiled=True)

    read = (
        height_now,
        zonal_now,
        ocean_depth,
        land_sea,
        meridional_now,
        metric,
        pinned(coriolis[None, :]),
        pinned(zonal_old),
        pinned(meridional_old),
    )
    held, arrived = loading(read)
    wet, zonal_part, meridional_part, green, solved, take, outer = call(
        local_kernel,
        [kept(columns, rows)] * 3
        + [pltpu.VMEM((3, rows, rows), BF16), kept(columns, rows), kept(blocks, 4, rows), kept(1, rows)],
        [HBM] * len(read) + [VMEM] * 4,
        [*held, arrived],
    )(*read, interim, vectors, alpha, beta)

    block = jax.ShapeDtypeStruct((columns, rows), F32)
    return tuple(
        call(finish_kernel, [block] * 3, [VMEM] * 10)(
            received, inner, outer, vectors, green, wet, zonal_part, meridional_part, solved, take
        )
    )


def solution(mesh):
    grid = P("lon", "lat")
    placed = (grid,) * 8 + (P("lat"), P("lat"), P(), P(), P(), P())
    return jax.shard_map(
        per_device, mesh=mesh, in_specs=placed, out_specs=(grid, grid, grid), check_vma=False
    )
```

```python
import jax
import jax.numpy as jnp
from jax import lax
from jax.experimental import pallas as pl
from jax.experimental.pallas import tpu as pltpu
from jax.sharding import PartitionSpec as P

COURANT = 0.25
F32 = jnp.float32
BF16 = jnp.bfloat16
HIGH = lax.Precision.HIGHEST
VMEM = pl.BlockSpec(memory_space=pltpu.VMEM)
HBM = pl.BlockSpec(memory_space=pltpu.HBM)
LIMIT = 8 << 20


def iota(shape, dim):
    return lax.broadcasted_iota(jnp.int32, shape, dim)


def dot(a, b, contract, precision=HIGH):
    return lax.dot_general(
        a, b, ((contract[:1], contract[1:]), ((), ())), precision=precision, preferred_element_type=F32
    )


def matmul2(x, y):
    a, b, c, d = x
    e, f, g, h = y
    return a * e + b * g, a * f + b * h, c * e + d * g, c * f + d * h


def product_scan(mats, axis, direction, rescale):
    shape = mats[0].shape
    size = shape[axis]
    place = iota(shape, axis)
    identity = (1.0, 0.0, 0.0, 1.0)
    step = 1
    while step < size:
        reach = [step * i for i in range(1, min(4, size // step))]
        others = []
        for distance in reach:
            if direction == 1:
                keep, shift = place >= distance, distance
            else:
                keep, shift = place < size - distance, size - distance
            others.append([jnp.where(keep, pltpu.roll(m, shift, axis), i) for m, i in zip(mats, identity)])
        factors = [mats, *others]
        while len(factors) > 1:
            factors = [matmul2(x, y) for x, y in zip(factors[::2], factors[1::2])]
        mats = factors[0]
        if rescale:
            factor = 1.0 / (mats[0] + mats[1] + mats[2] + mats[3])
            mats = tuple(m * factor for m in mats)
        step *= len(reach) + 1
    return mats


def lane(values, index):
    return jnp.broadcast_to(values[:, index : index + 1], values.shape)


def running_product(values, direction):
    size = values.shape[0]
    row = iota(values.shape, 0)
    step = 1
    while step < size:
        if direction == 1:
            keep, shift = row >= step, step
        else:
            keep, shift = row < size - step, size - step
        values = values * jnp.where(keep, pltpu.roll(values, shift, 0), 1.0)
        step *= 2
    return values


def differences(values, axis):
    size = values.shape[axis]
    place = iota(values.shape, axis)
    after = jnp.where(place == size - 1, 0.0, pltpu.roll(values, size - 1, axis))
    before = jnp.where(place == 0, 0.0, pltpu.roll(values, 1, axis))
    return after - before


def load(sources, held, arrived):
    copies = [pltpu.make_async_copy(src, dst, arrived.at[i]) for i, (src, dst) in enumerate(zip(sources, held))]
    for copy in copies:
        copy.start()
    return copies


def select_rows(row, parts):
    out = jnp.zeros(row.shape, F32)
    for index, part in enumerate(parts):
        out = jnp.where(row == index, part, out)
    return out


def thirds(values):
    high = values.astype(BF16).astype(F32)
    rest = values - high
    middle = rest.astype(BF16).astype(F32)
    return high, middle, rest - middle


def sums_dot(a, b):
    size = a.shape[0]
    left = jnp.concatenate(thirds(a), axis=0).astype(BF16)
    out = jnp.zeros((size, b.shape[0]), F32)
    for skip, part in enumerate(thirds(b)):
        product = dot(left, part.astype(BF16), (1, 1), None)
        for index in range(3 - skip):
            out += product[index * size : (index + 1) * size]
    return out


def sums_kernel(*refs):
    count = 14
    sources, refs = refs[:count], refs[count:]
    (
        own_ref,
        to_inner_ref,
        to_outer_ref,
        vectors_ref,
        wet_ref,
        zonal_part_ref,
        meridional_part_ref,
        green_ref,
        solved_ref,
        take_ref,
        outer_ref,
    ), refs = refs[:11], refs[11:]
    held, rows_ref, arrived = refs[:count], refs[count], refs[count + 1]
    copies = load(sources, held, arrived)
    (
        weight_ref,
        height_now_ref,
        zonal_ref,
        depth_ref,
        land_ref,
        lon_ref,
        lat_ref,
        amount_ref,
        meridional_ref,
        height_old_ref,
        metric_ref,
        coriolis_ref,
        zonal_old_ref,
        meridional_old_ref,
    ) = held
    columns, rows = height_now_ref.shape
    blocks = weight_ref.shape[0]
    block = lax.axis_index("lat")
    first_east = lax.axis_index("lon") * columns
    first_north = block * rows

    for copy in copies:
        copy.wait()
    c = 1.0 / weight_ref[...]
    one = jnp.ones_like(c)
    mats = (1.0 + c, one, c, one)
    up = product_scan(mats, 1, 1, False)
    down = product_scan(mats, 1, -1, False)
    up_all = tuple(lane(m, rows - 1) for m in up)
    down_all = tuple(lane(m, 0) for m in down)
    factor = 1.0 / (up_all[0] + up_all[1] + up_all[2] + up_all[3])
    ahead = product_scan(tuple(m * factor for m in up_all), 0, 1, True)
    factor = 1.0 / (down_all[0] + down_all[1] + down_all[2] + down_all[3])
    behind = product_scan(tuple(m * factor for m in down_all), 0, -1, True)
    row = iota(c.shape, 0)
    place = iota(c.shape, 1)
    rho = jnp.where(
        row == 0, 1.0, pltpu.roll((ahead[2] + ahead[3]) / (ahead[0] + ahead[1]), 1, 0)
    )
    sigma = jnp.where(
        row == blocks - 1,
        1.0,
        pltpu.roll((behind[2] + behind[3]) / (behind[0] + behind[1]), blocks - 1, 0),
    )
    p_after = up[0] + up[1] * rho
    q_before = down[0] + down[1] * sigma
    p = jnp.where(place == 0, 1.0, pltpu.roll(p_after, 1, 1))
    q = jnp.where(place == rows - 1, 1.0, pltpu.roll(q_before, rows - 1, 1))
    p_end = up_all[0] + up_all[1] * rho
    q_end = down_all[0] + down_all[1] * sigma
    scale = 1.0 / (up_all[2] + up_all[3] * rho + lane(p, rows - 1) * sigma)
    c_below = jnp.where(row == 0, 0.0, pltpu.roll(lane(c, rows - 1), 1, 0))
    c_above = jnp.where(row == blocks - 1, 0.0, pltpu.roll(lane(c, 0), blocks - 1, 0))
    low_p = -COURANT * c_below * (1.0 - rho)
    low_q = -COURANT * c_below * q_end
    high_p = COURANT * c_above * p_end
    high_q = COURANT * c_above * (1.0 - sigma)
    stacked = (
        p * c,
        q * c,
        q * scale,
        p * scale,
        low_p * q * scale,
        high_q * p * scale,
        jnp.where(place == 0, low_p, jnp.where(place == rows - 1, high_p, 0.0)),
        jnp.where(place == 0, low_q, jnp.where(place == rows - 1, high_q, 0.0)),
    )

    from_south = running_product(jnp.where(row < block, 1.0 / p_end, 1.0), -1)
    from_north = running_product(jnp.where(row > block, 1.0 / q_end, 1.0), 1)
    weights = (
        jnp.where(row < block, from_south, 0.0),
        jnp.where(row == block - 1, 1.0, 0.0),
        jnp.where(row > block, from_north, 0.0),
        jnp.where(row == block + 1, 1.0, 0.0),
    )
    for source in range(blocks):
        for index, values in enumerate(weights):
            take_ref[source, index : index + 1, :] = values[source : source + 1, :]
    for index, values in enumerate(stacked):
        rows_ref[index] = values
        vectors_ref[index : index + 1, :] = rows_ref[index, pl.ds(block, 1), :]

    shape = (columns, rows)
    subs = iota(shape, 0)
    lanes = iota(shape, 1)
    added = jnp.zeros(shape, F32)
    parts = thirds(amount_ref[...])
    chunks = range(lon_ref.shape[0])
    here = [lon_ref[i : i + 1, :] - first_east == subs for i in chunks]
    there = jnp.concatenate(
        [jnp.where(lat_ref[i : i + 1, :] - first_north == subs, 1.0, 0.0) for i in chunks], axis=1
    ).astype(BF16)
    for part in parts:
        amounts = jnp.concatenate([jnp.where(here[i], part[i : i + 1, :], 0.0) for i in chunks], axis=1)
        added += dot(amounts.astype(BF16), there, (1, 1), None)

    wet = land_ref[...].astype(F32)
    depth = depth_ref[...] * wet
    flux_east = depth * zonal_ref[...]
    flux_north = depth * meridional_ref[...]
    metric = metric_ref[...]
    interim = (
        height_old_ref[...]
        - COURANT * (metric * differences(flux_east, 0) + differences(flux_north, 1))
        + added
    )

    eight = iota((8, rows), 0)
    along = iota((8, rows), 1)
    vectors = vectors_ref[...]
    on_interim = jnp.where(eight < 2, vectors, 0.0)
    on_edges = jnp.where(eight < 2, pltpu.roll(vectors, 2, 0), 0.0)
    on_edges += jnp.where((eight == 2) & (along == 1) | (eight == 3) & (along == 2), 1.0, 0.0)
    edges = jnp.where((lanes == 0) | (lanes == rows - 1), flux_north, pltpu.roll(height_now_ref[...], 2, 1))
    total = sums_dot(
        jnp.concatenate([on_interim, on_edges], axis=1), jnp.concatenate([interim, edges], axis=1)
    )
    own_ref[...] = total[0:4]

    last = columns - 1
    odd = jnp.full((8, columns), lax.axis_index("lon") & 1, jnp.int32) == 1
    line = iota((8, columns), 1)
    onto = COURANT * metric * vectors
    flux_first, flux_last = flux_east[0:1, :], flux_east[last:columns, :]
    to_west = jnp.where(line == last, -jnp.sum(onto * flux_first, axis=1, keepdims=True), 0.0)
    to_east = jnp.where(line == 0, jnp.sum(onto * flux_last, axis=1, keepdims=True), 0.0)
    to_west = jnp.where(eight < 2, to_west, jnp.where(eight == 2, height_now_ref[0:1, :], flux_first))
    to_east = jnp.where(eight < 2, to_east, jnp.where(eight == 2, height_now_ref[last:columns, :], flux_last))
    to_inner_ref[...] = jnp.where(odd, to_west, to_east)[0:4]
    to_outer_ref[...] = jnp.where(odd, to_east, to_west)[0:4]

    p_from = jnp.broadcast_to(vectors[0:1, :], shape).T
    q_from = jnp.broadcast_to(vectors[1:2, :], shape).T
    green = thirds(jnp.where(subs <= lanes, p_from * vectors[2:3, :], q_from * vectors[3:4, :]))
    for index, part in enumerate(green):
        green_ref[index] = part.astype(BF16)
    parts = thirds(interim)
    pairs = [(i, j) for i in range(3) for j in range(3 - i)]
    solved = dot(
        jnp.concatenate([parts[i] for i, _ in pairs], axis=1).astype(BF16),
        jnp.concatenate([green[j] for _, j in pairs], axis=0).astype(BF16),
        (1, 0),
        None,
    )
    solved += flux_north[:, 0:1] * vectors[4:5, :] + flux_north[:, rows - 1 : rows] * vectors[5:6, :]
    solved_ref[...] = wet * solved

    height = height_now_ref[...]
    outer_ref[...] = COURANT * metric
    turning = coriolis_ref[...]
    wet_ref[...] = wet
    zonal_part_ref[...] = wet * (
        zonal_old_ref[...] - COURANT * metric * differences(height, 0) + turning * meridional_ref[...]
    )
    meridional_part_ref[...] = wet * (
        meridional_old_ref[...] - COURANT * differences(height, 1) - turning * zonal_ref[...]
    )


def pack_kernel(own_ref, inner_ref, to_outer_ref, send_ref):
    blocks = send_ref.shape[0] // 2
    block = lax.axis_index("lat")
    parity = lax.axis_index("lon") & 1
    at_own, at_outer = parity * blocks, (1 - parity) * blocks
    own = own_ref[...]
    row = iota(own.shape, 0)
    own += jnp.where(row < 2, inner_ref[1 - parity], 0.0)
    outer = to_outer_ref[...]
    own_up = jnp.concatenate([own[0:1], own[2:3]], axis=0)
    own_down = jnp.concatenate([own[1:2], own[3:4]], axis=0)
    outer_up = jnp.concatenate([outer[0:1], jnp.zeros_like(outer[0:1])], axis=0)
    outer_down = jnp.concatenate([outer[1:2], jnp.zeros_like(outer[0:1])], axis=0)
    for target in range(blocks):
        north = jnp.full(own_up.shape, (block < target).astype(jnp.int32), jnp.int32) == 1
        slot = blocks - 1 - target
        send_ref[at_own + slot] = jnp.where(north, own_up, own_down)
        send_ref[at_outer + slot] = jnp.where(north, outer_up, outer_down)
    send_ref[at_outer + blocks - 1 - block] = outer[2:4]


def finish_kernel(
    received_ref,
    inner_ref,
    outer_ref,
    vectors_ref,
    green_ref,
    wet_ref,
    zonal_part_ref,
    meridional_part_ref,
    solved_ref,
    take_ref,
    height_ref,
    zonal_ref,
    meridional_ref,
):
    columns, rows = wet_ref.shape
    blocks = take_ref.shape[0]
    last = columns - 1
    wet = wet_ref[...]
    outer = outer_ref[...]
    eight = iota((8, rows), 0)
    along = iota((8, columns), 1)
    block = lax.axis_index("lat")
    parity = lax.axis_index("lon") & 1
    at_own, at_other = parity * blocks, (1 - parity) * blocks

    inner = inner_ref[1 - parity][2:4]
    other = received_ref[at_other + blocks - 1 - block]
    odd = jnp.full(other.shape, parity, jnp.int32) == 1
    west = jnp.where(odd, inner, other)
    east = jnp.where(odd, other, inner)
    zonal_ref[...] = zonal_part_ref[...]
    zonal_ref[0:1, :] += wet_ref[0:1, :] * outer * west[0:1, :]
    zonal_ref[last:columns, :] -= wet_ref[last:columns, :] * outer * east[0:1, :]

    halo = select_rows(eight, (0.0, 0.0, 0.0, 0.0, outer * west[1:2, :], -outer * east[1:2, :]))
    left = jnp.concatenate(thirds(halo), axis=0).astype(BF16)
    outer_rows = jnp.zeros((8, rows), F32)
    for skip in range(3):
        product = dot(left, green_ref[skip], (1, 0), None)
        for index in range(3 - skip):
            outer_rows += product[8 * index : 8 * index + 8]

    south = jnp.zeros(other.shape, F32)
    north = jnp.zeros(other.shape, F32)
    for source in range(blocks):
        slot = blocks - 1 - source
        values = received_ref[at_own + slot] + received_ref[at_other + slot]
        take = take_ref[source]
        south += take[0:2] * values
        north += take[2:4] * values
    onto = jnp.concatenate([south, north, jnp.zeros((4, columns), F32)], axis=0)
    heights = select_rows(eight, (vectors_ref[2:3, :], 0.0, vectors_ref[3:4, :]))
    sides = jnp.where(
        (eight == 1) & (along == 0), COURANT, jnp.where((eight == 3) & (along == rows - 1), -COURANT, 0.0)
    )
    left = thirds(onto)
    right = thirds(jnp.concatenate([heights, sides], axis=1))
    pairs = [(i, j) for i in range(3) for j in range(3 - i)]
    both = dot(
        jnp.concatenate([left[i] for i, _ in pairs], axis=0).astype(BF16),
        jnp.concatenate([right[j] for _, j in pairs], axis=0).astype(BF16),
        (0, 0),
        None,
    )
    height_ref[...] = solved_ref[...] + wet * both[:, :rows]
    height_ref[0:1, :] += wet_ref[0:1, :] * outer_rows[4:5]
    height_ref[last:columns, :] += wet_ref[last:columns, :] * outer_rows[5:6]
    meridional_ref[...] = meridional_part_ref[...] + wet * both[:, rows:]


def call(kernel, outs, in_specs, scratch=()):
    return pl.pallas_call(
        kernel,
        out_shape=outs,
        in_specs=in_specs,
        out_specs=[VMEM] * len(outs),
        scratch_shapes=list(scratch),
        compiler_params=pltpu.CompilerParams(vmem_limit_bytes=LIMIT),
    )


def loading(read):
    return [pltpu.VMEM(x.shape, x.dtype) for x in read], pltpu.SemaphoreType.DMA((len(read),))


def kept(*shape):
    return pltpu.VMEM(shape, F32)


def per_device(
    height_old,
    height_now,
    zonal_old,
    zonal_now,
    meridional_old,
    meridional_now,
    ocean_depth,
    land_sea,
    metric_factor,
    coriolis,
    implicit_weight,
    source_longitude,
    source_latitude,
    source_amplitude,
):
    columns, rows = height_now.shape
    around = lax.axis_size("lon")
    blocks = lax.axis_size("lat")

    def pinned(values):
        return pltpu.with_memory_space_constraint(values, pltpu.HBM)

    read = (
        pinned(implicit_weight.reshape(blocks, rows)),
        pinned(height_now),
        pinned(zonal_now),
        pinned(ocean_depth),
        pinned(land_sea),
        pinned(source_longitude.reshape(-1, rows)),
        pinned(source_latitude.reshape(-1, rows)),
        pinned(source_amplitude.reshape(-1, rows)),
        pinned(meridional_now),
        pinned(height_old),
        pinned(metric_factor[None, :]),
        pinned(coriolis[None, :]),
        pinned(zonal_old),
        pinned(meridional_old),
    )
    held, arrived = loading(read)
    block = kept(columns, rows)
    own, to_inner, to_outer, vectors, wet, zonal_part, meridional_part, green, solved, take, outer = call(
        sums_kernel,
        [kept(4, columns), kept(4, columns), kept(4, columns), kept(8, rows), block, block, block]
        + [pltpu.VMEM((3, rows, rows), BF16), block, kept(blocks, 4, rows), kept(1, rows)],
        [HBM] * len(read),
        [*held, pltpu.VMEM((8, blocks, rows), F32), arrived],
    )(*read)

    pairs = [[i, i + 1] for i in range(0, around, 2)]
    inner = lax.all_gather(to_inner, "lon", axis=0, axis_index_groups=pairs)

    groups = [
        [lon * blocks + lat for lon in ((first + 1) % around, first) for lat in reversed(range(blocks))]
        for first in range(1, around, 2)
    ]
    (send,) = call(pack_kernel, [kept(2 * blocks, 2, columns)], [VMEM] * 3)(own, inner, to_outer)
    received = lax.all_to_all(send, ("lon", "lat"), 0, 0, axis_index_groups=groups, tiled=True)

    block = jax.ShapeDtypeStruct((columns, rows), F32)
    return tuple(
        call(finish_kernel, [block] * 3, [VMEM] * 10)(
            received, inner, outer, vectors, green, wet, zonal_part, meridional_part, solved, take
        )
    )


def solution(mesh):
    grid = P("lon", "lat")
    placed = (grid,) * 8 + (P("lat"), P("lat"), P(), P(), P(), P())
    return jax.shard_map(
        per_device, mesh=mesh, in_specs=placed, out_specs=(grid, grid, grid), check_vma=False
    )
```

```python
import jax
import jax.numpy as jnp
from jax import lax
from jax.experimental import pallas as pl
from jax.experimental.pallas import tpu as pltpu
from jax.sharding import PartitionSpec as P

COURANT = 0.25
F32 = jnp.float32
BF16 = jnp.bfloat16
HIGH = lax.Precision.HIGHEST
VMEM = pl.BlockSpec(memory_space=pltpu.VMEM)
HBM = pl.BlockSpec(memory_space=pltpu.HBM)
LIMIT = 8 << 20


def iota(shape, dim):
    return lax.broadcasted_iota(jnp.int32, shape, dim)


def dot(a, b, contract, precision=HIGH):
    return lax.dot_general(
        a, b, ((contract[:1], contract[1:]), ((), ())), precision=precision, preferred_element_type=F32
    )


def matmul2(x, y):
    a, b, c, d = x
    e, f, g, h = y
    return a * e + b * g, a * f + b * h, c * e + d * g, c * f + d * h


def product_scan(mats, axis, direction, rescale):
    shape = mats[0].shape
    size = shape[axis]
    place = iota(shape, axis)
    identity = (1.0, 0.0, 0.0, 1.0)
    step = 1
    while step < size:
        reach = [step * i for i in range(1, min(4, size // step))]
        others = []
        for distance in reach:
            if direction == 1:
                keep, shift = place >= distance, distance
            else:
                keep, shift = place < size - distance, size - distance
            others.append([jnp.where(keep, pltpu.roll(m, shift, axis), i) for m, i in zip(mats, identity)])
        factors = [mats, *others]
        while len(factors) > 1:
            factors = [matmul2(x, y) for x, y in zip(factors[::2], factors[1::2])]
        mats = factors[0]
        if rescale:
            factor = 1.0 / (mats[0] + mats[1] + mats[2] + mats[3])
            mats = tuple(m * factor for m in mats)
        step *= len(reach) + 1
    return mats


def lane(values, index):
    return jnp.broadcast_to(values[:, index : index + 1], values.shape)


def running_product(values, direction):
    size = values.shape[0]
    row = iota(values.shape, 0)
    step = 1
    while step < size:
        if direction == 1:
            keep, shift = row >= step, step
        else:
            keep, shift = row < size - step, size - step
        values = values * jnp.where(keep, pltpu.roll(values, shift, 0), 1.0)
        step *= 2
    return values


def differences(values, axis):
    size = values.shape[axis]
    place = iota(values.shape, axis)
    after = jnp.where(place == size - 1, 0.0, pltpu.roll(values, size - 1, axis))
    before = jnp.where(place == 0, 0.0, pltpu.roll(values, 1, axis))
    return after - before


def load(sources, held, arrived):
    copies = [pltpu.make_async_copy(src, dst, arrived.at[i]) for i, (src, dst) in enumerate(zip(sources, held))]
    for copy in copies:
        copy.start()
    return copies


def select_rows(row, parts):
    out = jnp.zeros(row.shape, F32)
    for index, part in enumerate(parts):
        out = jnp.where(row == index, part, out)
    return out


def thirds(values):
    high = values.astype(BF16).astype(F32)
    rest = values - high
    middle = rest.astype(BF16).astype(F32)
    return high, middle, rest - middle


def sums_dot(a, b):
    size = a.shape[0]
    left = jnp.concatenate(thirds(a), axis=0).astype(BF16)
    out = jnp.zeros((size, b.shape[0]), F32)
    for skip, part in enumerate(thirds(b)):
        product = dot(left, part.astype(BF16), (1, 1), None)
        for index in range(3 - skip):
            out += product[index * size : (index + 1) * size]
    return out


def sums_kernel(*refs):
    count = 14
    sources, refs = refs[:count], refs[count:]
    (
        own_ref,
        to_inner_ref,
        to_outer_ref,
        vectors_ref,
        wet_ref,
        zonal_part_ref,
        meridional_part_ref,
        green_ref,
        solved_ref,
        take_ref,
        outer_ref,
    ), refs = refs[:11], refs[11:]
    held, rows_ref, arrived = refs[:count], refs[count], refs[count + 1]
    copies = load(sources, held, arrived)
    (
        weight_ref,
        height_now_ref,
        zonal_ref,
        depth_ref,
        land_ref,
        lon_ref,
        lat_ref,
        amount_ref,
        meridional_ref,
        height_old_ref,
        metric_ref,
        coriolis_ref,
        zonal_old_ref,
        meridional_old_ref,
    ) = held
    columns, rows = height_now_ref.shape
    blocks = weight_ref.shape[0]
    block = lax.axis_index("lat")
    first_east = lax.axis_index("lon") * columns
    first_north = block * rows

    for copy in copies:
        copy.wait()
    c = 1.0 / weight_ref[...]
    one = jnp.ones_like(c)
    mats = (1.0 + c, one, c, one)
    up = product_scan(mats, 1, 1, False)
    down = product_scan(mats, 1, -1, False)
    up_all = tuple(lane(m, rows - 1) for m in up)
    down_all = tuple(lane(m, 0) for m in down)
    factor = 1.0 / (up_all[0] + up_all[1] + up_all[2] + up_all[3])
    ahead = product_scan(tuple(m * factor for m in up_all), 0, 1, True)
    factor = 1.0 / (down_all[0] + down_all[1] + down_all[2] + down_all[3])
    behind = product_scan(tuple(m * factor for m in down_all), 0, -1, True)
    row = iota(c.shape, 0)
    place = iota(c.shape, 1)
    rho = jnp.where(
        row == 0, 1.0, pltpu.roll((ahead[2] + ahead[3]) / (ahead[0] + ahead[1]), 1, 0)
    )
    sigma = jnp.where(
        row == blocks - 1,
        1.0,
        pltpu.roll((behind[2] + behind[3]) / (behind[0] + behind[1]), blocks - 1, 0),
    )
    p_after = up[0] + up[1] * rho
    q_before = down[0] + down[1] * sigma
    p = jnp.where(place == 0, 1.0, pltpu.roll(p_after, 1, 1))
    q = jnp.where(place == rows - 1, 1.0, pltpu.roll(q_before, rows - 1, 1))
    p_end = up_all[0] + up_all[1] * rho
    q_end = down_all[0] + down_all[1] * sigma
    scale = 1.0 / (up_all[2] + up_all[3] * rho + lane(p, rows - 1) * sigma)
    c_below = jnp.where(row == 0, 0.0, pltpu.roll(lane(c, rows - 1), 1, 0))
    c_above = jnp.where(row == blocks - 1, 0.0, pltpu.roll(lane(c, 0), blocks - 1, 0))
    low_p = -COURANT * c_below * (1.0 - rho)
    low_q = -COURANT * c_below * q_end
    high_p = COURANT * c_above * p_end
    high_q = COURANT * c_above * (1.0 - sigma)
    stacked = (
        p * c,
        q * c,
        q * scale,
        p * scale,
        low_p * q * scale,
        high_q * p * scale,
        jnp.where(place == 0, low_p, jnp.where(place == rows - 1, high_p, 0.0)),
        jnp.where(place == 0, low_q, jnp.where(place == rows - 1, high_q, 0.0)),
    )

    from_south = running_product(jnp.where(row < block, 1.0 / p_end, 1.0), -1)
    from_north = running_product(jnp.where(row > block, 1.0 / q_end, 1.0), 1)
    weights = (
        jnp.where(row < block, from_south, 0.0),
        jnp.where(row == block - 1, 1.0, 0.0),
        jnp.where(row > block, from_north, 0.0),
        jnp.where(row == block + 1, 1.0, 0.0),
    )
    for source in range(blocks):
        for index, values in enumerate(weights):
            take_ref[source, index : index + 1, :] = values[source : source + 1, :]
    for index, values in enumerate(stacked):
        rows_ref[index] = values
        vectors_ref[index : index + 1, :] = rows_ref[index, pl.ds(block, 1), :]

    shape = (columns, rows)
    subs = iota(shape, 0)
    lanes = iota(shape, 1)
    added = jnp.zeros(shape, F32)
    parts = thirds(amount_ref[...])
    chunks = range(lon_ref.shape[0])
    here = [lon_ref[i : i + 1, :] - first_east == subs for i in chunks]
    there = jnp.concatenate(
        [jnp.where(lat_ref[i : i + 1, :] - first_north == subs, 1.0, 0.0) for i in chunks], axis=1
    ).astype(BF16)
    for part in parts:
        amounts = jnp.concatenate([jnp.where(here[i], part[i : i + 1, :], 0.0) for i in chunks], axis=1)
        added += dot(amounts.astype(BF16), there, (1, 1), None)

    wet = land_ref[...].astype(F32)
    depth = depth_ref[...] * wet
    flux_east = depth * zonal_ref[...]
    flux_north = depth * meridional_ref[...]
    metric = metric_ref[...]
    interim = (
        height_old_ref[...]
        - COURANT * (metric * differences(flux_east, 0) + differences(flux_north, 1))
        + added
    )

    eight = iota((8, rows), 0)
    along = iota((8, rows), 1)
    vectors = vectors_ref[...]
    on_interim = jnp.where(eight < 2, vectors, 0.0)
    on_edges = jnp.where(eight < 2, pltpu.roll(vectors, 2, 0), 0.0)
    on_edges += jnp.where((eight == 2) & (along == 1) | (eight == 3) & (along == 2), 1.0, 0.0)
    edges = jnp.where((lanes == 0) | (lanes == rows - 1), flux_north, pltpu.roll(height_now_ref[...], 2, 1))
    total = sums_dot(
        jnp.concatenate([on_interim, on_edges], axis=1), jnp.concatenate([interim, edges], axis=1)
    )
    own_ref[...] = total[0:4]

    last = columns - 1
    odd = jnp.full((8, columns), lax.axis_index("lon") & 1, jnp.int32) == 1
    line = iota((8, columns), 1)
    onto = COURANT * metric * vectors
    flux_first, flux_last = flux_east[0:1, :], flux_east[last:columns, :]
    to_west = jnp.where(line == last, -jnp.sum(onto * flux_first, axis=1, keepdims=True), 0.0)
    to_east = jnp.where(line == 0, jnp.sum(onto * flux_last, axis=1, keepdims=True), 0.0)
    to_west = jnp.where(eight < 2, to_west, jnp.where(eight == 2, height_now_ref[0:1, :], flux_first))
    to_east = jnp.where(eight < 2, to_east, jnp.where(eight == 2, height_now_ref[last:columns, :], flux_last))
    to_inner_ref[...] = jnp.where(odd, to_west, to_east)[0:4]
    to_outer_ref[...] = jnp.where(odd, to_east, to_west)[0:4]

    p_from = jnp.broadcast_to(vectors[0:1, :], shape).T
    q_from = jnp.broadcast_to(vectors[1:2, :], shape).T
    green = thirds(jnp.where(subs <= lanes, p_from * vectors[2:3, :], q_from * vectors[3:4, :]))
    for index, part in enumerate(green):
        green_ref[index] = part.astype(BF16)
    parts = thirds(interim)
    pairs = [(i, j) for i in range(3) for j in range(3 - i)]
    solved = dot(
        jnp.concatenate([parts[i] for i, _ in pairs], axis=1).astype(BF16),
        jnp.concatenate([green[j] for _, j in pairs], axis=0).astype(BF16),
        (1, 0),
        None,
    )
    solved += flux_north[:, 0:1] * vectors[4:5, :] + flux_north[:, rows - 1 : rows] * vectors[5:6, :]
    solved_ref[...] = wet * solved

    height = height_now_ref[...]
    outer_ref[...] = COURANT * metric
    turning = coriolis_ref[...]
    wet_ref[...] = wet
    zonal_part_ref[...] = wet * (
        zonal_old_ref[...] - COURANT * metric * differences(height, 0) + turning * meridional_ref[...]
    )
    meridional_part_ref[...] = wet * (
        meridional_old_ref[...] - COURANT * differences(height, 1) - turning * zonal_ref[...]
    )


def pack_kernel(own_ref, inner_ref, to_outer_ref, send_ref):
    blocks = send_ref.shape[0] // 2
    block = lax.axis_index("lat")
    parity = lax.axis_index("lon") & 1
    own = own_ref[...]
    row = iota(own.shape, 0)
    own += jnp.where(row < 2, inner_ref[1 - parity], 0.0)
    outer = to_outer_ref[...]
    own_up = jnp.concatenate([own[0:1], own[2:3]], axis=0)
    own_down = jnp.concatenate([own[1:2], own[3:4]], axis=0)
    outer_up = jnp.concatenate([outer[0:1], jnp.zeros_like(outer[0:1])], axis=0)
    outer_down = jnp.concatenate([outer[1:2], jnp.zeros_like(outer[0:1])], axis=0)
    for target in range(blocks):
        north = jnp.full(own_up.shape, (block < target).astype(jnp.int32), jnp.int32) == 1
        slot = 2 * (blocks - 1 - target)
        send_ref[slot + 1 - parity] = jnp.where(north, own_up, own_down)
        send_ref[slot + parity] = jnp.where(north, outer_up, outer_down)
    send_ref[2 * (blocks - 1 - block) + parity] = outer[2:4]


def finish_kernel(
    received_ref,
    inner_ref,
    outer_ref,
    vectors_ref,
    green_ref,
    wet_ref,
    zonal_part_ref,
    meridional_part_ref,
    solved_ref,
    take_ref,
    height_ref,
    zonal_ref,
    meridional_ref,
):
    columns, rows = wet_ref.shape
    blocks = take_ref.shape[0]
    last = columns - 1
    wet = wet_ref[...]
    outer = outer_ref[...]
    eight = iota((8, rows), 0)
    along = iota((8, columns), 1)
    block = lax.axis_index("lat")
    parity = lax.axis_index("lon") & 1

    inner = inner_ref[1 - parity][2:4]
    other = received_ref[2 * (blocks - 1 - block) + parity]
    odd = jnp.full(other.shape, parity, jnp.int32) == 1
    west = jnp.where(odd, inner, other)
    east = jnp.where(odd, other, inner)
    zonal_ref[...] = zonal_part_ref[...]
    zonal_ref[0:1, :] += wet_ref[0:1, :] * outer * west[0:1, :]
    zonal_ref[last:columns, :] -= wet_ref[last:columns, :] * outer * east[0:1, :]

    halo = select_rows(eight, (0.0, 0.0, 0.0, 0.0, outer * west[1:2, :], -outer * east[1:2, :]))
    left = jnp.concatenate(thirds(halo), axis=0).astype(BF16)
    outer_rows = jnp.zeros((8, rows), F32)
    for skip in range(3):
        product = dot(left, green_ref[skip], (1, 0), None)
        for index in range(3 - skip):
            outer_rows += product[8 * index : 8 * index + 8]

    south = jnp.zeros(other.shape, F32)
    north = jnp.zeros(other.shape, F32)
    for source in range(blocks):
        slot = 2 * (blocks - 1 - source)
        values = received_ref[slot] + received_ref[slot + 1]
        take = take_ref[source]
        south += take[0:2] * values
        north += take[2:4] * values
    onto = jnp.concatenate([south, north, jnp.zeros((4, columns), F32)], axis=0)
    heights = select_rows(eight, (vectors_ref[2:3, :], 0.0, vectors_ref[3:4, :]))
    sides = jnp.where(
        (eight == 1) & (along == 0), COURANT, jnp.where((eight == 3) & (along == rows - 1), -COURANT, 0.0)
    )
    left = thirds(onto)
    right = thirds(jnp.concatenate([heights, sides], axis=1))
    pairs = [(i, j) for i in range(3) for j in range(3 - i)]
    both = dot(
        jnp.concatenate([left[i] for i, _ in pairs], axis=0).astype(BF16),
        jnp.concatenate([right[j] for _, j in pairs], axis=0).astype(BF16),
        (0, 0),
        None,
    )
    height_ref[...] = solved_ref[...] + wet * both[:, :rows]
    height_ref[0:1, :] += wet_ref[0:1, :] * outer_rows[4:5]
    height_ref[last:columns, :] += wet_ref[last:columns, :] * outer_rows[5:6]
    meridional_ref[...] = meridional_part_ref[...] + wet * both[:, rows:]


def call(kernel, outs, in_specs, scratch=()):
    return pl.pallas_call(
        kernel,
        out_shape=outs,
        in_specs=in_specs,
        out_specs=[VMEM] * len(outs),
        scratch_shapes=list(scratch),
        compiler_params=pltpu.CompilerParams(vmem_limit_bytes=LIMIT),
    )


def loading(read):
    return [pltpu.VMEM(x.shape, x.dtype) for x in read], pltpu.SemaphoreType.DMA((len(read),))


def kept(*shape):
    return pltpu.VMEM(shape, F32)


def per_device(
    height_old,
    height_now,
    zonal_old,
    zonal_now,
    meridional_old,
    meridional_now,
    ocean_depth,
    land_sea,
    metric_factor,
    coriolis,
    implicit_weight,
    source_longitude,
    source_latitude,
    source_amplitude,
):
    columns, rows = height_now.shape
    around = lax.axis_size("lon")
    blocks = lax.axis_size("lat")

    def pinned(values):
        return pltpu.with_memory_space_constraint(values, pltpu.HBM)

    read = (
        pinned(implicit_weight.reshape(blocks, rows)),
        pinned(height_now),
        pinned(zonal_now),
        pinned(ocean_depth),
        pinned(land_sea),
        pinned(source_longitude.reshape(-1, rows)),
        pinned(source_latitude.reshape(-1, rows)),
        pinned(source_amplitude.reshape(-1, rows)),
        pinned(meridional_now),
        pinned(height_old),
        pinned(metric_factor[None, :]),
        pinned(coriolis[None, :]),
        pinned(zonal_old),
        pinned(meridional_old),
    )
    held, arrived = loading(read)
    block = kept(columns, rows)
    own, to_inner, to_outer, vectors, wet, zonal_part, meridional_part, green, solved, take, outer = call(
        sums_kernel,
        [kept(4, columns), kept(4, columns), kept(4, columns), kept(8, rows), block, block, block]
        + [pltpu.VMEM((3, rows, rows), BF16), block, kept(blocks, 4, rows), kept(1, rows)],
        [HBM] * len(read),
        [*held, pltpu.VMEM((8, blocks, rows), F32), arrived],
    )(*read)

    pairs = [[i, i + 1] for i in range(0, around, 2)]
    inner = lax.all_gather(to_inner, "lon", axis=0, axis_index_groups=pairs)

    groups = [
        [lon * blocks + lat for lat in reversed(range(blocks)) for lon in (first, (first + 1) % around)]
        for first in range(1, around, 2)
    ]
    (send,) = call(pack_kernel, [kept(2 * blocks, 2, columns)], [VMEM] * 3)(own, inner, to_outer)
    received = lax.all_to_all(send, ("lon", "lat"), 0, 0, axis_index_groups=groups, tiled=True)

    block = jax.ShapeDtypeStruct((columns, rows), F32)
    return tuple(
        call(finish_kernel, [block] * 3, [VMEM] * 10)(
            received, inner, outer, vectors, green, wet, zonal_part, meridional_part, solved, take
        )
    )


def solution(mesh):
    grid = P("lon", "lat")
    placed = (grid,) * 8 + (P("lat"), P("lat"), P(), P(), P(), P())
    return jax.shard_map(
        per_device, mesh=mesh, in_specs=placed, out_specs=(grid, grid, grid), check_vma=False
    )
```

```python
import jax
import jax.numpy as jnp
from jax import lax
from jax.experimental import pallas as pl
from jax.experimental.pallas import tpu as pltpu
from jax.sharding import PartitionSpec as P

COURANT = 0.25
F32 = jnp.float32
BF16 = jnp.bfloat16
HIGH = lax.Precision.HIGHEST
VMEM = pl.BlockSpec(memory_space=pltpu.VMEM)
HBM = pl.BlockSpec(memory_space=pltpu.HBM)
LIMIT = 8 << 20


def iota(shape, dim):
    return lax.broadcasted_iota(jnp.int32, shape, dim)


def dot(a, b, contract, precision=HIGH):
    return lax.dot_general(
        a, b, ((contract[:1], contract[1:]), ((), ())), precision=precision, preferred_element_type=F32
    )


def matmul2(x, y):
    a, b, c, d = x
    e, f, g, h = y
    return a * e + b * g, a * f + b * h, c * e + d * g, c * f + d * h


def product_scan(mats, axis, direction, rescale):
    shape = mats[0].shape
    size = shape[axis]
    place = iota(shape, axis)
    identity = (1.0, 0.0, 0.0, 1.0)
    step = 1
    while step < size:
        reach = [step * i for i in range(1, min(4, size // step))]
        others = []
        for distance in reach:
            if direction == 1:
                keep, shift = place >= distance, distance
            else:
                keep, shift = place < size - distance, size - distance
            others.append([jnp.where(keep, pltpu.roll(m, shift, axis), i) for m, i in zip(mats, identity)])
        factors = [mats, *others]
        while len(factors) > 1:
            factors = [matmul2(x, y) for x, y in zip(factors[::2], factors[1::2])]
        mats = factors[0]
        if rescale:
            factor = 1.0 / (mats[0] + mats[1] + mats[2] + mats[3])
            mats = tuple(m * factor for m in mats)
        step *= len(reach) + 1
    return mats


def lane(values, index):
    return jnp.broadcast_to(values[:, index : index + 1], values.shape)


def running_product(values, direction):
    size = values.shape[0]
    row = iota(values.shape, 0)
    step = 1
    while step < size:
        if direction == 1:
            keep, shift = row >= step, step
        else:
            keep, shift = row < size - step, size - step
        values = values * jnp.where(keep, pltpu.roll(values, shift, 0), 1.0)
        step *= 2
    return values


def differences(values, axis):
    size = values.shape[axis]
    place = iota(values.shape, axis)
    after = jnp.where(place == size - 1, 0.0, pltpu.roll(values, size - 1, axis))
    before = jnp.where(place == 0, 0.0, pltpu.roll(values, 1, axis))
    return after - before


def place(lat, blocks):
    half = blocks // 2
    if isinstance(lat, int):
        return (2 * (blocks - 1 - lat), 1) if lat >= half else (blocks + half - 1 - lat, half)
    north = lat >= half
    return jnp.where(north, 2 * (blocks - 1 - lat), blocks + half - 1 - lat), jnp.where(north, 1, half)


def load(sources, held, arrived):
    copies = [pltpu.make_async_copy(src, dst, arrived.at[i]) for i, (src, dst) in enumerate(zip(sources, held))]
    for copy in copies:
        copy.start()
    return copies


def select_rows(row, parts):
    out = jnp.zeros(row.shape, F32)
    for index, part in enumerate(parts):
        out = jnp.where(row == index, part, out)
    return out


def thirds(values):
    high = values.astype(BF16).astype(F32)
    rest = values - high
    middle = rest.astype(BF16).astype(F32)
    return high, middle, rest - middle


def sums_dot(a, b):
    size = a.shape[0]
    left = jnp.concatenate(thirds(a), axis=0).astype(BF16)
    out = jnp.zeros((size, b.shape[0]), F32)
    for skip, part in enumerate(thirds(b)):
        product = dot(left, part.astype(BF16), (1, 1), None)
        for index in range(3 - skip):
            out += product[index * size : (index + 1) * size]
    return out


def sums_kernel(*refs):
    count = 14
    sources, refs = refs[:count], refs[count:]
    (
        own_ref,
        to_inner_ref,
        to_outer_ref,
        vectors_ref,
        wet_ref,
        zonal_part_ref,
        meridional_part_ref,
        green_ref,
        solved_ref,
        take_ref,
        outer_ref,
    ), refs = refs[:11], refs[11:]
    held, rows_ref, arrived = refs[:count], refs[count], refs[count + 1]
    copies = load(sources, held, arrived)
    (
        weight_ref,
        height_now_ref,
        zonal_ref,
        depth_ref,
        land_ref,
        lon_ref,
        lat_ref,
        amount_ref,
        meridional_ref,
        height_old_ref,
        metric_ref,
        coriolis_ref,
        zonal_old_ref,
        meridional_old_ref,
    ) = held
    columns, rows = height_now_ref.shape
    blocks = weight_ref.shape[0]
    block = lax.axis_index("lat")
    first_east = lax.axis_index("lon") * columns
    first_north = block * rows

    for copy in copies:
        copy.wait()
    c = 1.0 / weight_ref[...]
    one = jnp.ones_like(c)
    mats = (1.0 + c, one, c, one)
    up = product_scan(mats, 1, 1, False)
    down = product_scan(mats, 1, -1, False)
    up_all = tuple(lane(m, rows - 1) for m in up)
    down_all = tuple(lane(m, 0) for m in down)
    factor = 1.0 / (up_all[0] + up_all[1] + up_all[2] + up_all[3])
    ahead = product_scan(tuple(m * factor for m in up_all), 0, 1, True)
    factor = 1.0 / (down_all[0] + down_all[1] + down_all[2] + down_all[3])
    behind = product_scan(tuple(m * factor for m in down_all), 0, -1, True)
    row = iota(c.shape, 0)
    place = iota(c.shape, 1)
    rho = jnp.where(
        row == 0, 1.0, pltpu.roll((ahead[2] + ahead[3]) / (ahead[0] + ahead[1]), 1, 0)
    )
    sigma = jnp.where(
        row == blocks - 1,
        1.0,
        pltpu.roll((behind[2] + behind[3]) / (behind[0] + behind[1]), blocks - 1, 0),
    )
    p_after = up[0] + up[1] * rho
    q_before = down[0] + down[1] * sigma
    p = jnp.where(place == 0, 1.0, pltpu.roll(p_after, 1, 1))
    q = jnp.where(place == rows - 1, 1.0, pltpu.roll(q_before, rows - 1, 1))
    p_end = up_all[0] + up_all[1] * rho
    q_end = down_all[0] + down_all[1] * sigma
    scale = 1.0 / (up_all[2] + up_all[3] * rho + lane(p, rows - 1) * sigma)
    c_below = jnp.where(row == 0, 0.0, pltpu.roll(lane(c, rows - 1), 1, 0))
    c_above = jnp.where(row == blocks - 1, 0.0, pltpu.roll(lane(c, 0), blocks - 1, 0))
    low_p = -COURANT * c_below * (1.0 - rho)
    low_q = -COURANT * c_below * q_end
    high_p = COURANT * c_above * p_end
    high_q = COURANT * c_above * (1.0 - sigma)
    stacked = (
        p * c,
        q * c,
        q * scale,
        p * scale,
        low_p * q * scale,
        high_q * p * scale,
        jnp.where(place == 0, low_p, jnp.where(place == rows - 1, high_p, 0.0)),
        jnp.where(place == 0, low_q, jnp.where(place == rows - 1, high_q, 0.0)),
    )

    from_south = running_product(jnp.where(row < block, 1.0 / p_end, 1.0), -1)
    from_north = running_product(jnp.where(row > block, 1.0 / q_end, 1.0), 1)
    weights = (
        jnp.where(row < block, from_south, 0.0),
        jnp.where(row == block - 1, 1.0, 0.0),
        jnp.where(row > block, from_north, 0.0),
        jnp.where(row == block + 1, 1.0, 0.0),
    )
    for source in range(blocks):
        for index, values in enumerate(weights):
            take_ref[source, index : index + 1, :] = values[source : source + 1, :]
    for index, values in enumerate(stacked):
        rows_ref[index] = values
        vectors_ref[index : index + 1, :] = rows_ref[index, pl.ds(block, 1), :]

    shape = (columns, rows)
    subs = iota(shape, 0)
    lanes = iota(shape, 1)
    added = jnp.zeros(shape, F32)
    parts = thirds(amount_ref[...])
    chunks = range(lon_ref.shape[0])
    here = [lon_ref[i : i + 1, :] - first_east == subs for i in chunks]
    there = jnp.concatenate(
        [jnp.where(lat_ref[i : i + 1, :] - first_north == subs, 1.0, 0.0) for i in chunks], axis=1
    ).astype(BF16)
    for part in parts:
        amounts = jnp.concatenate([jnp.where(here[i], part[i : i + 1, :], 0.0) for i in chunks], axis=1)
        added += dot(amounts.astype(BF16), there, (1, 1), None)

    wet = land_ref[...].astype(F32)
    depth = depth_ref[...] * wet
    flux_east = depth * zonal_ref[...]
    flux_north = depth * meridional_ref[...]
    metric = metric_ref[...]
    interim = (
        height_old_ref[...]
        - COURANT * (metric * differences(flux_east, 0) + differences(flux_north, 1))
        + added
    )

    eight = iota((8, rows), 0)
    along = iota((8, rows), 1)
    vectors = vectors_ref[...]
    on_interim = jnp.where(eight < 2, vectors, 0.0)
    on_edges = jnp.where(eight < 2, pltpu.roll(vectors, 2, 0), 0.0)
    on_edges += jnp.where((eight == 2) & (along == 1) | (eight == 3) & (along == 2), 1.0, 0.0)
    edges = jnp.where((lanes == 0) | (lanes == rows - 1), flux_north, pltpu.roll(height_now_ref[...], 2, 1))
    total = sums_dot(
        jnp.concatenate([on_interim, on_edges], axis=1), jnp.concatenate([interim, edges], axis=1)
    )
    own_ref[...] = total[0:4]

    last = columns - 1
    odd = jnp.full((8, columns), lax.axis_index("lon") & 1, jnp.int32) == 1
    line = iota((8, columns), 1)
    onto = COURANT * metric * vectors
    flux_first, flux_last = flux_east[0:1, :], flux_east[last:columns, :]
    to_west = jnp.where(line == last, -jnp.sum(onto * flux_first, axis=1, keepdims=True), 0.0)
    to_east = jnp.where(line == 0, jnp.sum(onto * flux_last, axis=1, keepdims=True), 0.0)
    to_west = jnp.where(eight < 2, to_west, jnp.where(eight == 2, height_now_ref[0:1, :], flux_first))
    to_east = jnp.where(eight < 2, to_east, jnp.where(eight == 2, height_now_ref[last:columns, :], flux_last))
    to_inner_ref[...] = jnp.where(odd, to_west, to_east)[0:4]
    to_outer_ref[...] = jnp.where(odd, to_east, to_west)[0:4]

    p_from = jnp.broadcast_to(vectors[0:1, :], shape).T
    q_from = jnp.broadcast_to(vectors[1:2, :], shape).T
    green = thirds(jnp.where(subs <= lanes, p_from * vectors[2:3, :], q_from * vectors[3:4, :]))
    for index, part in enumerate(green):
        green_ref[index] = part.astype(BF16)
    parts = thirds(interim)
    pairs = [(i, j) for i in range(3) for j in range(3 - i)]
    solved = dot(
        jnp.concatenate([parts[i] for i, _ in pairs], axis=1).astype(BF16),
        jnp.concatenate([green[j] for _, j in pairs], axis=0).astype(BF16),
        (1, 0),
        None,
    )
    solved += flux_north[:, 0:1] * vectors[4:5, :] + flux_north[:, rows - 1 : rows] * vectors[5:6, :]
    solved_ref[...] = wet * solved

    height = height_now_ref[...]
    outer_ref[...] = COURANT * metric
    turning = coriolis_ref[...]
    wet_ref[...] = wet
    zonal_part_ref[...] = wet * (
        zonal_old_ref[...] - COURANT * metric * differences(height, 0) + turning * meridional_ref[...]
    )
    meridional_part_ref[...] = wet * (
        meridional_old_ref[...] - COURANT * differences(height, 1) - turning * zonal_ref[...]
    )


def pack_kernel(own_ref, inner_ref, to_outer_ref, send_ref):
    blocks = send_ref.shape[0] // 2
    block = lax.axis_index("lat")
    parity = lax.axis_index("lon") & 1
    own = own_ref[...]
    row = iota(own.shape, 0)
    own += jnp.where(row < 2, inner_ref[1 - parity], 0.0)
    outer = to_outer_ref[...]
    own_up = jnp.concatenate([own[0:1], own[2:3]], axis=0)
    own_down = jnp.concatenate([own[1:2], own[3:4]], axis=0)
    outer_up = jnp.concatenate([outer[0:1], jnp.zeros_like(outer[0:1])], axis=0)
    outer_down = jnp.concatenate([outer[1:2], jnp.zeros_like(outer[0:1])], axis=0)
    for target in range(blocks):
        north = jnp.full(own_up.shape, (block < target).astype(jnp.int32), jnp.int32) == 1
        slot, step = place(target, blocks)
        send_ref[slot + step * parity] = jnp.where(north, own_up, own_down)
        send_ref[slot + step * (1 - parity)] = jnp.where(north, outer_up, outer_down)
    slot, step = place(block, blocks)
    send_ref[slot + step * (1 - parity)] = outer[2:4]


def finish_kernel(
    received_ref,
    inner_ref,
    outer_ref,
    vectors_ref,
    green_ref,
    wet_ref,
    zonal_part_ref,
    meridional_part_ref,
    solved_ref,
    take_ref,
    height_ref,
    zonal_ref,
    meridional_ref,
):
    columns, rows = wet_ref.shape
    blocks = take_ref.shape[0]
    last = columns - 1
    wet = wet_ref[...]
    outer = outer_ref[...]
    eight = iota((8, rows), 0)
    along = iota((8, columns), 1)
    block = lax.axis_index("lat")
    parity = lax.axis_index("lon") & 1
    slot, step = place(block, blocks)

    inner = inner_ref[1 - parity][2:4]
    other = received_ref[slot + step * (1 - parity)]
    odd = jnp.full(other.shape, parity, jnp.int32) == 1
    west = jnp.where(odd, inner, other)
    east = jnp.where(odd, other, inner)
    zonal_ref[...] = zonal_part_ref[...]
    zonal_ref[0:1, :] += wet_ref[0:1, :] * outer * west[0:1, :]
    zonal_ref[last:columns, :] -= wet_ref[last:columns, :] * outer * east[0:1, :]

    halo = select_rows(eight, (0.0, 0.0, 0.0, 0.0, outer * west[1:2, :], -outer * east[1:2, :]))
    left = jnp.concatenate(thirds(halo), axis=0).astype(BF16)
    outer_rows = jnp.zeros((8, rows), F32)
    for skip in range(3):
        product = dot(left, green_ref[skip], (1, 0), None)
        for index in range(3 - skip):
            outer_rows += product[8 * index : 8 * index + 8]

    south = jnp.zeros(other.shape, F32)
    north = jnp.zeros(other.shape, F32)
    for source in range(blocks):
        slot, step = place(source, blocks)
        values = received_ref[slot] + received_ref[slot + step]
        take = take_ref[source]
        south += take[0:2] * values
        north += take[2:4] * values
    onto = jnp.concatenate([south, north, jnp.zeros((4, columns), F32)], axis=0)
    heights = select_rows(eight, (vectors_ref[2:3, :], 0.0, vectors_ref[3:4, :]))
    sides = jnp.where(
        (eight == 1) & (along == 0), COURANT, jnp.where((eight == 3) & (along == rows - 1), -COURANT, 0.0)
    )
    left = thirds(onto)
    right = thirds(jnp.concatenate([heights, sides], axis=1))
    pairs = [(i, j) for i in range(3) for j in range(3 - i)]
    both = dot(
        jnp.concatenate([left[i] for i, _ in pairs], axis=0).astype(BF16),
        jnp.concatenate([right[j] for _, j in pairs], axis=0).astype(BF16),
        (0, 0),
        None,
    )
    height_ref[...] = solved_ref[...] + wet * both[:, :rows]
    height_ref[0:1, :] += wet_ref[0:1, :] * outer_rows[4:5]
    height_ref[last:columns, :] += wet_ref[last:columns, :] * outer_rows[5:6]
    meridional_ref[...] = meridional_part_ref[...] + wet * both[:, rows:]


def call(kernel, outs, in_specs, scratch=()):
    return pl.pallas_call(
        kernel,
        out_shape=outs,
        in_specs=in_specs,
        out_specs=[VMEM] * len(outs),
        scratch_shapes=list(scratch),
        compiler_params=pltpu.CompilerParams(vmem_limit_bytes=LIMIT),
    )


def loading(read):
    return [pltpu.VMEM(x.shape, x.dtype) for x in read], pltpu.SemaphoreType.DMA((len(read),))


def kept(*shape):
    return pltpu.VMEM(shape, F32)


def per_device(
    height_old,
    height_now,
    zonal_old,
    zonal_now,
    meridional_old,
    meridional_now,
    ocean_depth,
    land_sea,
    metric_factor,
    coriolis,
    implicit_weight,
    source_longitude,
    source_latitude,
    source_amplitude,
):
    columns, rows = height_now.shape
    around = lax.axis_size("lon")
    blocks = lax.axis_size("lat")

    def pinned(values):
        return pltpu.with_memory_space_constraint(values, pltpu.HBM)

    read = (
        pinned(implicit_weight.reshape(blocks, rows)),
        pinned(height_now),
        pinned(zonal_now),
        pinned(ocean_depth),
        pinned(land_sea),
        pinned(source_longitude.reshape(-1, rows)),
        pinned(source_latitude.reshape(-1, rows)),
        pinned(source_amplitude.reshape(-1, rows)),
        pinned(meridional_now),
        pinned(height_old),
        pinned(metric_factor[None, :]),
        pinned(coriolis[None, :]),
        pinned(zonal_old),
        pinned(meridional_old),
    )
    held, arrived = loading(read)
    block = kept(columns, rows)
    own, to_inner, to_outer, vectors, wet, zonal_part, meridional_part, green, solved, take, outer = call(
        sums_kernel,
        [kept(4, columns), kept(4, columns), kept(4, columns), kept(8, rows), block, block, block]
        + [pltpu.VMEM((3, rows, rows), BF16), block, kept(blocks, 4, rows), kept(1, rows)],
        [HBM] * len(read),
        [*held, pltpu.VMEM((8, blocks, rows), F32), arrived],
    )(*read)

    pairs = [[i, i + 1] for i in range(0, around, 2)]
    inner = lax.all_gather(to_inner, "lon", axis=0, axis_index_groups=pairs)

    members = [(odd, lat) for lat in range(blocks) for odd in (0, 1)]
    members.sort(key=lambda m: place(m[1], blocks)[0] + place(m[1], blocks)[1] * m[0])
    groups = [
        [(first + 1 - odd) % around * blocks + lat for odd, lat in members]
        for first in range(1, around, 2)
    ]
    (send,) = call(pack_kernel, [kept(2 * blocks, 2, columns)], [VMEM] * 3)(own, inner, to_outer)
    received = lax.all_to_all(send, ("lon", "lat"), 0, 0, axis_index_groups=groups, tiled=True)

    block = jax.ShapeDtypeStruct((columns, rows), F32)
    return tuple(
        call(finish_kernel, [block] * 3, [VMEM] * 10)(
            received, inner, outer, vectors, green, wet, zonal_part, meridional_part, solved, take
        )
    )


def solution(mesh):
    grid = P("lon", "lat")
    placed = (grid,) * 8 + (P("lat"), P("lat"), P(), P(), P(), P())
    return jax.shard_map(
        per_device, mesh=mesh, in_specs=placed, out_specs=(grid, grid, grid), check_vma=False
    )
```

```python
import jax
import jax.numpy as jnp
from jax import lax
from jax.experimental import pallas as pl
from jax.experimental.pallas import tpu as pltpu
from jax.sharding import PartitionSpec as P

COURANT = 0.25
F32 = jnp.float32
BF16 = jnp.bfloat16
HIGH = lax.Precision.HIGHEST
VMEM = pl.BlockSpec(memory_space=pltpu.VMEM)
HBM = pl.BlockSpec(memory_space=pltpu.HBM)
LIMIT = 8 << 20


def iota(shape, dim):
    return lax.broadcasted_iota(jnp.int32, shape, dim)


def dot(a, b, contract, precision=HIGH):
    return lax.dot_general(
        a, b, ((contract[:1], contract[1:]), ((), ())), precision=precision, preferred_element_type=F32
    )


def matmul2(x, y):
    a, b, c, d = x
    e, f, g, h = y
    return a * e + b * g, a * f + b * h, c * e + d * g, c * f + d * h


def product_scan(mats, axis, direction, rescale):
    shape = mats[0].shape
    size = shape[axis]
    place = iota(shape, axis)
    identity = (1.0, 0.0, 0.0, 1.0)
    step = 1
    while step < size:
        reach = [step * i for i in range(1, min(4, size // step))]
        others = []
        for distance in reach:
            if direction == 1:
                keep, shift = place >= distance, distance
            else:
                keep, shift = place < size - distance, size - distance
            others.append([jnp.where(keep, pltpu.roll(m, shift, axis), i) for m, i in zip(mats, identity)])
        factors = [mats, *others]
        while len(factors) > 1:
            factors = [matmul2(x, y) for x, y in zip(factors[::2], factors[1::2])]
        mats = factors[0]
        if rescale:
            factor = 1.0 / (mats[0] + mats[1] + mats[2] + mats[3])
            mats = tuple(m * factor for m in mats)
        step *= len(reach) + 1
    return mats


def lane(values, index):
    return jnp.broadcast_to(values[:, index : index + 1], values.shape)


def running_product(values, direction):
    size = values.shape[0]
    row = iota(values.shape, 0)
    step = 1
    while step < size:
        if direction == 1:
            keep, shift = row >= step, step
        else:
            keep, shift = row < size - step, size - step
        values = values * jnp.where(keep, pltpu.roll(values, shift, 0), 1.0)
        step *= 2
    return values


def differences(values, axis):
    size = values.shape[axis]
    place = iota(values.shape, axis)
    after = jnp.where(place == size - 1, 0.0, pltpu.roll(values, size - 1, axis))
    before = jnp.where(place == 0, 0.0, pltpu.roll(values, 1, axis))
    return after - before


def place(lat, blocks):
    half = blocks // 2
    if isinstance(lat, int):
        return (2 * (blocks - 1 - lat), 1) if lat >= half else (blocks + half - 1 - lat, half)
    north = lat >= half
    return jnp.where(north, 2 * (blocks - 1 - lat), blocks + half - 1 - lat), jnp.where(north, 1, half)


def load(sources, held, arrived):
    copies = [pltpu.make_async_copy(src, dst, arrived.at[i]) for i, (src, dst) in enumerate(zip(sources, held))]
    for copy in copies:
        copy.start()
    return copies


def select_rows(row, parts):
    out = jnp.zeros(row.shape, F32)
    for index, part in enumerate(parts):
        out = jnp.where(row == index, part, out)
    return out


def thirds(values):
    high = values.astype(BF16).astype(F32)
    rest = values - high
    middle = rest.astype(BF16).astype(F32)
    return high, middle, rest - middle


def sums_dot(a, b):
    size = a.shape[0]
    left = jnp.concatenate(thirds(a), axis=0).astype(BF16)
    out = jnp.zeros((size, b.shape[0]), F32)
    for skip, part in enumerate(thirds(b)):
        product = dot(left, part.astype(BF16), (1, 1), None)
        for index in range(3 - skip):
            out += product[index * size : (index + 1) * size]
    return out


def sums_kernel(*refs):
    count = 14
    sources, refs = refs[:count], refs[count:]
    (
        own_ref,
        to_inner_ref,
        to_outer_ref,
        vectors_ref,
        wet_ref,
        zonal_part_ref,
        meridional_part_ref,
        green_ref,
        solved_ref,
        take_ref,
        outer_ref,
    ), refs = refs[:11], refs[11:]
    held, rows_ref, arrived = refs[:count], refs[count], refs[count + 1]
    copies = load(sources, held, arrived)
    (
        weight_ref,
        height_now_ref,
        zonal_ref,
        depth_ref,
        land_ref,
        lon_ref,
        lat_ref,
        amount_ref,
        meridional_ref,
        height_old_ref,
        metric_ref,
        coriolis_ref,
        zonal_old_ref,
        meridional_old_ref,
    ) = held
    columns, rows = height_now_ref.shape
    blocks = weight_ref.shape[0]
    block = lax.axis_index("lat")
    first_east = lax.axis_index("lon") * columns
    first_north = block * rows

    copies[0].wait()
    c = 1.0 / weight_ref[...]
    one = jnp.ones_like(c)
    mats = (1.0 + c, one, c, one)
    up = product_scan(mats, 1, 1, False)
    down = product_scan(mats, 1, -1, False)
    up_all = tuple(lane(m, rows - 1) for m in up)
    down_all = tuple(lane(m, 0) for m in down)
    factor = 1.0 / (up_all[0] + up_all[1] + up_all[2] + up_all[3])
    ahead = product_scan(tuple(m * factor for m in up_all), 0, 1, True)
    factor = 1.0 / (down_all[0] + down_all[1] + down_all[2] + down_all[3])
    behind = product_scan(tuple(m * factor for m in down_all), 0, -1, True)
    row = iota(c.shape, 0)
    place = iota(c.shape, 1)
    rho = jnp.where(
        row == 0, 1.0, pltpu.roll((ahead[2] + ahead[3]) / (ahead[0] + ahead[1]), 1, 0)
    )
    sigma = jnp.where(
        row == blocks - 1,
        1.0,
        pltpu.roll((behind[2] + behind[3]) / (behind[0] + behind[1]), blocks - 1, 0),
    )
    p_after = up[0] + up[1] * rho
    q_before = down[0] + down[1] * sigma
    p = jnp.where(place == 0, 1.0, pltpu.roll(p_after, 1, 1))
    q = jnp.where(place == rows - 1, 1.0, pltpu.roll(q_before, rows - 1, 1))
    p_end = up_all[0] + up_all[1] * rho
    q_end = down_all[0] + down_all[1] * sigma
    scale = 1.0 / (up_all[2] + up_all[3] * rho + lane(p, rows - 1) * sigma)
    c_below = jnp.where(row == 0, 0.0, pltpu.roll(lane(c, rows - 1), 1, 0))
    c_above = jnp.where(row == blocks - 1, 0.0, pltpu.roll(lane(c, 0), blocks - 1, 0))
    low_p = -COURANT * c_below * (1.0 - rho)
    low_q = -COURANT * c_below * q_end
    high_p = COURANT * c_above * p_end
    high_q = COURANT * c_above * (1.0 - sigma)
    stacked = (
        p * c,
        q * c,
        q * scale,
        p * scale,
        low_p * q * scale,
        high_q * p * scale,
        jnp.where(place == 0, low_p, jnp.where(place == rows - 1, high_p, 0.0)),
        jnp.where(place == 0, low_q, jnp.where(place == rows - 1, high_q, 0.0)),
    )

    from_south = running_product(jnp.where(row < block, 1.0 / p_end, 1.0), -1)
    from_north = running_product(jnp.where(row > block, 1.0 / q_end, 1.0), 1)
    weights = (
        jnp.where(row < block, from_south, 0.0),
        jnp.where(row == block - 1, 1.0, 0.0),
        jnp.where(row > block, from_north, 0.0),
        jnp.where(row == block + 1, 1.0, 0.0),
    )
    for source in range(blocks):
        for index, values in enumerate(weights):
            take_ref[source, index : index + 1, :] = values[source : source + 1, :]
    for index, values in enumerate(stacked):
        rows_ref[index] = values
        vectors_ref[index : index + 1, :] = rows_ref[index, pl.ds(block, 1), :]

    for copy in copies[1:]:
        copy.wait()
    shape = (columns, rows)
    subs = iota(shape, 0)
    lanes = iota(shape, 1)
    added = jnp.zeros(shape, F32)
    parts = thirds(amount_ref[...])
    chunks = range(lon_ref.shape[0])
    here = [lon_ref[i : i + 1, :] - first_east == subs for i in chunks]
    there = jnp.concatenate(
        [jnp.where(lat_ref[i : i + 1, :] - first_north == subs, 1.0, 0.0) for i in chunks], axis=1
    ).astype(BF16)
    for part in parts:
        amounts = jnp.concatenate([jnp.where(here[i], part[i : i + 1, :], 0.0) for i in chunks], axis=1)
        added += dot(amounts.astype(BF16), there, (1, 1), None)

    wet = land_ref[...].astype(F32)
    depth = depth_ref[...] * wet
    flux_east = depth * zonal_ref[...]
    flux_north = depth * meridional_ref[...]
    metric = metric_ref[...]
    interim = (
        height_old_ref[...]
        - COURANT * (metric * differences(flux_east, 0) + differences(flux_north, 1))
        + added
    )

    eight = iota((8, rows), 0)
    along = iota((8, rows), 1)
    vectors = vectors_ref[...]
    on_interim = jnp.where(eight < 2, vectors, 0.0)
    on_edges = jnp.where(eight < 2, pltpu.roll(vectors, 2, 0), 0.0)
    on_edges += jnp.where((eight == 2) & (along == 1) | (eight == 3) & (along == 2), 1.0, 0.0)
    edges = jnp.where((lanes == 0) | (lanes == rows - 1), flux_north, pltpu.roll(height_now_ref[...], 2, 1))
    total = sums_dot(
        jnp.concatenate([on_interim, on_edges], axis=1), jnp.concatenate([interim, edges], axis=1)
    )
    own_ref[...] = total[0:4]

    last = columns - 1
    odd = jnp.full((8, columns), lax.axis_index("lon") & 1, jnp.int32) == 1
    line = iota((8, columns), 1)
    onto = COURANT * metric * vectors
    flux_first, flux_last = flux_east[0:1, :], flux_east[last:columns, :]
    to_west = jnp.where(line == last, -jnp.sum(onto * flux_first, axis=1, keepdims=True), 0.0)
    to_east = jnp.where(line == 0, jnp.sum(onto * flux_last, axis=1, keepdims=True), 0.0)
    to_west = jnp.where(eight < 2, to_west, jnp.where(eight == 2, height_now_ref[0:1, :], flux_first))
    to_east = jnp.where(eight < 2, to_east, jnp.where(eight == 2, height_now_ref[last:columns, :], flux_last))
    to_inner_ref[...] = jnp.where(odd, to_west, to_east)[0:4]
    to_outer_ref[...] = jnp.where(odd, to_east, to_west)[0:4]

    p_from = jnp.broadcast_to(vectors[0:1, :], shape).T
    q_from = jnp.broadcast_to(vectors[1:2, :], shape).T
    green = thirds(jnp.where(subs <= lanes, p_from * vectors[2:3, :], q_from * vectors[3:4, :]))
    for index, part in enumerate(green):
        green_ref[index] = part.astype(BF16)
    parts = thirds(interim)
    pairs = [(i, j) for i in range(3) for j in range(3 - i)]
    solved = dot(
        jnp.concatenate([parts[i] for i, _ in pairs], axis=1).astype(BF16),
        jnp.concatenate([green[j] for _, j in pairs], axis=0).astype(BF16),
        (1, 0),
        None,
    )
    solved += flux_north[:, 0:1] * vectors[4:5, :] + flux_north[:, rows - 1 : rows] * vectors[5:6, :]
    solved_ref[...] = wet * solved

    height = height_now_ref[...]
    outer_ref[...] = COURANT * metric
    turning = coriolis_ref[...]
    wet_ref[...] = wet
    zonal_part_ref[...] = wet * (
        zonal_old_ref[...] - COURANT * metric * differences(height, 0) + turning * meridional_ref[...]
    )
    meridional_part_ref[...] = wet * (
        meridional_old_ref[...] - COURANT * differences(height, 1) - turning * zonal_ref[...]
    )


def pack_kernel(own_ref, inner_ref, to_outer_ref, send_ref):
    blocks = send_ref.shape[0] // 2
    block = lax.axis_index("lat")
    parity = lax.axis_index("lon") & 1
    own = own_ref[...]
    row = iota(own.shape, 0)
    own += jnp.where(row < 2, inner_ref[1 - parity], 0.0)
    outer = to_outer_ref[...]
    own_up = jnp.concatenate([own[0:1], own[2:3]], axis=0)
    own_down = jnp.concatenate([own[1:2], own[3:4]], axis=0)
    outer_up = jnp.concatenate([outer[0:1], jnp.zeros_like(outer[0:1])], axis=0)
    outer_down = jnp.concatenate([outer[1:2], jnp.zeros_like(outer[0:1])], axis=0)
    for target in range(blocks):
        north = jnp.full(own_up.shape, (block < target).astype(jnp.int32), jnp.int32) == 1
        slot, step = place(target, blocks)
        send_ref[slot + step * parity] = jnp.where(north, own_up, own_down)
        send_ref[slot + step * (1 - parity)] = jnp.where(north, outer_up, outer_down)
    slot, step = place(block, blocks)
    send_ref[slot + step * (1 - parity)] = outer[2:4]


def finish_kernel(
    received_ref,
    inner_ref,
    outer_ref,
    vectors_ref,
    green_ref,
    wet_ref,
    zonal_part_ref,
    meridional_part_ref,
    solved_ref,
    take_ref,
    height_ref,
    zonal_ref,
    meridional_ref,
):
    columns, rows = wet_ref.shape
    blocks = take_ref.shape[0]
    last = columns - 1
    wet = wet_ref[...]
    outer = outer_ref[...]
    eight = iota((8, rows), 0)
    along = iota((8, columns), 1)
    block = lax.axis_index("lat")
    parity = lax.axis_index("lon") & 1
    slot, step = place(block, blocks)

    inner = inner_ref[1 - parity][2:4]
    other = received_ref[slot + step * (1 - parity)]
    odd = jnp.full(other.shape, parity, jnp.int32) == 1
    west = jnp.where(odd, inner, other)
    east = jnp.where(odd, other, inner)
    zonal_ref[...] = zonal_part_ref[...]
    zonal_ref[0:1, :] += wet_ref[0:1, :] * outer * west[0:1, :]
    zonal_ref[last:columns, :] -= wet_ref[last:columns, :] * outer * east[0:1, :]

    halo = select_rows(eight, (0.0, 0.0, 0.0, 0.0, outer * west[1:2, :], -outer * east[1:2, :]))
    left = jnp.concatenate(thirds(halo), axis=0).astype(BF16)
    outer_rows = jnp.zeros((8, rows), F32)
    for skip in range(3):
        product = dot(left, green_ref[skip], (1, 0), None)
        for index in range(3 - skip):
            outer_rows += product[8 * index : 8 * index + 8]

    south = jnp.zeros(other.shape, F32)
    north = jnp.zeros(other.shape, F32)
    for source in range(blocks):
        slot, step = place(source, blocks)
        values = received_ref[slot] + received_ref[slot + step]
        take = take_ref[source]
        south += take[0:2] * values
        north += take[2:4] * values
    onto = jnp.concatenate([south, north, jnp.zeros((4, columns), F32)], axis=0)
    heights = select_rows(eight, (vectors_ref[2:3, :], 0.0, vectors_ref[3:4, :]))
    sides = jnp.where(
        (eight == 1) & (along == 0), COURANT, jnp.where((eight == 3) & (along == rows - 1), -COURANT, 0.0)
    )
    left = thirds(onto)
    right = thirds(jnp.concatenate([heights, sides], axis=1))
    pairs = [(i, j) for i in range(3) for j in range(3 - i)]
    both = dot(
        jnp.concatenate([left[i] for i, _ in pairs], axis=0).astype(BF16),
        jnp.concatenate([right[j] for _, j in pairs], axis=0).astype(BF16),
        (0, 0),
        None,
    )
    height_ref[...] = solved_ref[...] + wet * both[:, :rows]
    height_ref[0:1, :] += wet_ref[0:1, :] * outer_rows[4:5]
    height_ref[last:columns, :] += wet_ref[last:columns, :] * outer_rows[5:6]
    meridional_ref[...] = meridional_part_ref[...] + wet * both[:, rows:]


def call(kernel, outs, in_specs, scratch=()):
    return pl.pallas_call(
        kernel,
        out_shape=outs,
        in_specs=in_specs,
        out_specs=[VMEM] * len(outs),
        scratch_shapes=list(scratch),
        compiler_params=pltpu.CompilerParams(vmem_limit_bytes=LIMIT),
    )


def loading(read):
    return [pltpu.VMEM(x.shape, x.dtype) for x in read], pltpu.SemaphoreType.DMA((len(read),))


def kept(*shape):
    return pltpu.VMEM(shape, F32)


def per_device(
    height_old,
    height_now,
    zonal_old,
    zonal_now,
    meridional_old,
    meridional_now,
    ocean_depth,
    land_sea,
    metric_factor,
    coriolis,
    implicit_weight,
    source_longitude,
    source_latitude,
    source_amplitude,
):
    columns, rows = height_now.shape
    around = lax.axis_size("lon")
    blocks = lax.axis_size("lat")

    def pinned(values):
        return pltpu.with_memory_space_constraint(values, pltpu.HBM)

    read = (
        pinned(implicit_weight.reshape(blocks, rows)),
        pinned(height_now),
        pinned(zonal_now),
        pinned(ocean_depth),
        pinned(land_sea),
        pinned(source_longitude.reshape(-1, rows)),
        pinned(source_latitude.reshape(-1, rows)),
        pinned(source_amplitude.reshape(-1, rows)),
        pinned(meridional_now),
        pinned(height_old),
        pinned(metric_factor[None, :]),
        pinned(coriolis[None, :]),
        pinned(zonal_old),
        pinned(meridional_old),
    )
    held, arrived = loading(read)
    block = kept(columns, rows)
    own, to_inner, to_outer, vectors, wet, zonal_part, meridional_part, green, solved, take, outer = call(
        sums_kernel,
        [kept(4, columns), kept(4, columns), kept(4, columns), kept(8, rows), block, block, block]
        + [pltpu.VMEM((3, rows, rows), BF16), block, kept(blocks, 4, rows), kept(1, rows)],
        [HBM] * len(read),
        [*held, pltpu.VMEM((8, blocks, rows), F32), arrived],
    )(*read)

    pairs = [[i, i + 1] for i in range(0, around, 2)]
    inner = lax.all_gather(to_inner, "lon", axis=0, axis_index_groups=pairs)

    members = [(odd, lat) for lat in range(blocks) for odd in (0, 1)]
    members.sort(key=lambda m: place(m[1], blocks)[0] + place(m[1], blocks)[1] * m[0])
    groups = [
        [(first + 1 - odd) % around * blocks + lat for odd, lat in members]
        for first in range(1, around, 2)
    ]
    (send,) = call(pack_kernel, [kept(2 * blocks, 2, columns)], [VMEM] * 3)(own, inner, to_outer)
    received = lax.all_to_all(send, ("lon", "lat"), 0, 0, axis_index_groups=groups, tiled=True)

    block = jax.ShapeDtypeStruct((columns, rows), F32)
    return tuple(
        call(finish_kernel, [block] * 3, [VMEM] * 10)(
            received, inner, outer, vectors, green, wet, zonal_part, meridional_part, solved, take
        )
    )


def solution(mesh):
    grid = P("lon", "lat")
    placed = (grid,) * 8 + (P("lat"), P("lat"), P(), P(), P(), P())
    return jax.shard_map(
        per_device, mesh=mesh, in_specs=placed, out_specs=(grid, grid, grid), check_vma=False
    )
```
